256 devices in a mesh: dp: 2 (over x_lo), ctx: 16 (over z, core), exp: 8 (over y, x_hi).
Axes of the slice: x: 4 (x_hi: 2, x_lo: 2; x = x_hi * 2 + x_lo), y: 4, z: 8, core: 2. Of those that a mesh axis runs over, the one named last changes fastest.
Arguments:
- queries: bfloat16 [512, 6144], P(('dp', 'ctx'), 'exp'), parts along dimension 0, may hold values from -150 to 150
- span_keys: bfloat16 [512, 1024], P(('dp', 'ctx'), 'exp'), parts along dimension 0, may hold values from -5 to 5
- span_values: bfloat16 [512, 1024], P(('dp', 'ctx'), 'exp'), parts along dimension 0, may hold values from -5 to 5
- cache_keys: bfloat16 [131072, 1024], P(('dp', 'ctx'), 'exp'), parts along dimension 0, may hold values from -5 to 5
- cache_values: bfloat16 [131072, 1024], P(('dp', 'ctx'), 'exp'), parts along dimension 0, may hold values from -5 to 5
- span_start: int32 [2], P('dp'), parts along dimension 0, may hold values from 16384 to 65536
- residual: bfloat16 [512, 6144], P(('dp', 'ctx', 'exp')), parts along dimension 0, may hold values from -40 to 40
- out_weight: bfloat16 [6144, 6144], P('exp', 'ctx'), may hold values from -0.078125 to 0.078125
- norm_gain: bfloat16 [6144], replicated, may hold values from 0.099609375 to 1.8984375
- router_weight: bfloat16 [6144, 4], replicated, may hold values from -0.078125 to 0.078125
- expert_ids: int32 [512, 2], P('dp'), parts along dimension 0, may hold values from 0 to 3, as said below
- gate_weight: bfloat16 [6144, 32768], P(None, ('ctx', 'exp')), may hold values from -0.078125 to 0.078125
- up_weight: bfloat16 [6144, 32768], P(None, ('ctx', 'exp')), may hold values from -0.078125 to 0.078125
- down_weight: bfloat16 [32768, 6144], P(('ctx', 'exp')), may hold values from -0.0625 to 0.0625
Outputs:
- mixed: bfloat16 [512, 6144], P(('dp', 'ctx', 'exp')), parts along dimension 0
The draws below stay inside these ranges and needn't reach their ends.
There are 2 independent parts, one for each index of `dp`. The reference program is written for one: setup_inputs(seed, part) draws one part's arguments, and reference() takes and returns one part's arrays. A program takes and returns all parts, laid end to end along the dimension named above; an argument that names none is the same for every part. Nothing has to cross between parts.
Inputs may be any that keep to these rules, and one draw needn't show every extreme that they name: `expert_ids`: the two experts of a token differ.
All inputs are finite; a program needn't handle non-finite values.
Results may differ from the reference program's by a relative error of at most 0.013.
Values may be sent and summed in bfloat16 or wider, within the bound.
No kernel may reach another device: no remote copies, remote signals or barrier semaphores. Data moves between devices by JAX's collectives and lax.ppermute only.
A program may use at most 128 MiB of HBM per device.

```python
import math
import jax
import jax.numpy as jnp
from jax import lax

D = 6144
HEADS = 48
KV_HEADS = 8
HEAD_DIM = 128
EXPERTS = 4
FF = 8192
TOPK = 2
SPAN = 256
CACHE = 65536
CAP = 160


def shared_keys(key):
    return jnp.clip(jax.random.normal(key, (CACHE, KV_HEADS * HEAD_DIM), jnp.float32), -5.0, 5.0)


def draw_cache_keys(key, part):
    values = shared_keys(key)
    return values.astype(jnp.bfloat16)


def draw_queries(key, part):
    folded = jax.random.fold_in(key, 2)
    values = jnp.clip(3.0 * jax.random.normal(folded, (SPAN, HEADS * HEAD_DIM), jnp.float32), -18.0, 18.0)
    return values.astype(jnp.bfloat16)


def draw_residual(key, part):
    folded = jax.random.fold_in(key, 3)
    row_scale = jnp.exp(jax.random.uniform(jax.random.fold_in(folded, 1), (SPAN, 1), jnp.float32, math.log(0.5), math.log(5.0)))
    col_scale = jnp.exp(jax.random.uniform(jax.random.fold_in(folded, 2), (1, D), jnp.float32, math.log(0.5), math.log(2.0)))
    core = jnp.clip(jax.random.normal(jax.random.fold_in(folded, 3), (SPAN, D), jnp.float32), -4.0, 4.0)
    return (core * row_scale * col_scale).astype(jnp.bfloat16)


def draw_expert_ids(key, part):
    folded = jax.random.fold_in(key, 4)
    favoured = jax.random.randint(jax.random.fold_in(folded, 1), (), 0, EXPERTS)
    favoured_count = jax.random.randint(jax.random.fold_in(folded, 2), (), 11 * SPAN // 16, 7 * SPAN // 8 + 1)
    shuffled = jax.random.permutation(jax.random.fold_in(folded, 3), SPAN)
    position_of = jnp.argsort(shuffled)
    has_favoured = position_of < favoured_count
    partner = (favoured + jax.random.randint(jax.random.fold_in(folded, 4), (SPAN,), 1, EXPERTS)) % EXPERTS
    first_pick = jax.random.randint(jax.random.fold_in(folded, 5), (SPAN,), 0, EXPERTS - 1)
    second_step = jax.random.randint(jax.random.fold_in(folded, 6), (SPAN,), 1, EXPERTS - 1)
    first_other = (favoured + 1 + first_pick) % EXPERTS
    second_other = (favoured + 1 + (first_pick + second_step) % (EXPERTS - 1)) % EXPERTS
    column_one = jnp.where(has_favoured, favoured, first_other)
    column_two = jnp.where(has_favoured, partner, second_other)
    flipped = jax.random.randint(jax.random.fold_in(folded, 7), (SPAN,), 0, 2) == 1
    leading = jnp.where(flipped, column_two, column_one)
    trailing = jnp.where(flipped, column_one, column_two)
    return jnp.stack([leading, trailing], axis=1).astype(jnp.int32)


def block_scale(key, dims, cuts, low, top_value):
    loudness = 1.0
    for position, parts in cuts:
        heights = jax.random.uniform(jax.random.fold_in(jax.random.fold_in(key, 6), position), (parts,), jnp.float32, low / len(cuts), top_value / len(cuts))
        loudness = loudness * jnp.repeat(jnp.exp(heights), dims[position] // parts).reshape((-1,) + (1,) * (len(dims) - 1 - position))
    return loudness


def noise(stream_key, shape, deviation, limit, pieces=(), kind=jnp.bfloat16):
    drawn = jax.random.normal(stream_key, shape, jnp.float32) * deviation
    if len(pieces) > 0:
        drawn = block_scale(stream_key, shape, pieces, -0.22, 0.18) * drawn
    return jnp.clip(drawn, min=-limit, max=limit).astype(kind)


def setup_inputs(seed: int = 0, part: int = 0) -> dict:
    key_list = jax.random.split(jax.random.key(seed), 15)
    part_splits = jax.random.split(jax.random.fold_in(key_list[14], part), 15)
    queries = draw_queries(jax.random.fold_in(jax.random.fold_in(key_list[14], part), 71), part)
    span_keys = noise(part_splits[1], (SPAN, KV_HEADS * HEAD_DIM), 1.0, 5.0, ((0, 16), (1, 8)))
    span_values = noise(part_splits[2], (SPAN, KV_HEADS * HEAD_DIM), 1.0, 5.0, ((0, 16), (1, 8)))
    cache_keys = draw_cache_keys(jax.random.fold_in(jax.random.fold_in(key_list[14], part), 71), part)
    cache_values = noise(part_splits[4], (CACHE, KV_HEADS * HEAD_DIM), 1.0, 5.0, ((0, 16), (1, 8)))
    span_start = jax.random.randint(part_splits[5], (1,), CACHE // 4, CACHE + 1).astype(jnp.int32)
    residual = draw_residual(jax.random.fold_in(jax.random.fold_in(key_list[14], part), 71), part)
    out_weight = noise(key_list[7], (HEADS * HEAD_DIM, D), (HEADS * HEAD_DIM) ** -0.5, 0.078125, ((0, 8), (1, 16)))
    norm_gain = jnp.clip(1.0 + 0.18 * jax.random.normal(key_list[8], (D,), jnp.float32), 0.099609375, 1.8984375).astype(jnp.bfloat16)
    router_weight = noise(key_list[9], (D, EXPERTS), D ** -0.5, 0.078125)
    expert_ids = draw_expert_ids(jax.random.fold_in(jax.random.fold_in(key_list[14], part), 71), part)
    gate_weight = noise(key_list[11], (D, EXPERTS * FF), D ** -0.5, 0.078125, ((1, 128),))
    up_weight = noise(key_list[12], (D, EXPERTS * FF), D ** -0.5, 0.078125, ((1, 128),))
    down_weight = noise(key_list[13], (EXPERTS * FF, D), FF ** -0.5, 0.0625, ((0, 128),))
    return dict(queries=queries, span_keys=span_keys, span_values=span_values, cache_keys=cache_keys, cache_values=cache_values, span_start=span_start, residual=residual, out_weight=out_weight, norm_gain=norm_gain, router_weight=router_weight, expert_ids=expert_ids, gate_weight=gate_weight, up_weight=up_weight, down_weight=down_weight)


EPSILON = 1e-05
MASKED = -1e+30

def reference(queries, span_keys, span_values, cache_keys, cache_values, span_start, residual, out_weight, norm_gain, router_weight, expert_ids, gate_weight, up_weight, down_weight):
    per_group = HEADS // KV_HEADS
    key_total = CACHE + SPAN
    row_block = math.gcd(SPAN, 128)
    all_keys = jnp.concatenate([cache_keys, span_keys], axis=0).reshape(key_total, KV_HEADS, HEAD_DIM)
    all_values = jnp.concatenate([cache_values, span_values], axis=0).reshape(key_total, KV_HEADS, HEAD_DIM)
    query_heads = queries.reshape(SPAN, KV_HEADS, per_group, HEAD_DIM)
    cache_live = jnp.arange(CACHE, dtype=jnp.int32) < span_start[0]
    causal = jnp.arange(SPAN, dtype=jnp.int32)[None, :] <= jnp.arange(SPAN, dtype=jnp.int32)[:, None]
    allowed = jnp.concatenate([jnp.broadcast_to(cache_live[None, :], (SPAN, CACHE)), causal], axis=1)

    def group_attention(group_no):
        group_keys = lax.dynamic_index_in_dim(all_keys, group_no, 1, keepdims=False)
        group_values = lax.dynamic_index_in_dim(all_values, group_no, 1, keepdims=False)
        group_queries = lax.dynamic_index_in_dim(query_heads, group_no, 1, keepdims=False)

        def block_attention(block_no):
            first = block_no * row_block
            block_queries = lax.dynamic_slice_in_dim(group_queries, first, row_block, 0).reshape(row_block * per_group, HEAD_DIM)
            block_allowed = lax.dynamic_slice_in_dim(allowed, first, row_block, 0)
            scores = jnp.dot(block_queries, group_keys.T, preferred_element_type=jnp.float32) * HEAD_DIM ** (-0.5)
            scores = scores.reshape(row_block, per_group, key_total)
            scores = jnp.where(block_allowed[:, None, :], scores, MASKED)
            peaks = lax.optimization_barrier(jnp.max(scores, axis=2, keepdims=True))
            weights = jnp.where(block_allowed[:, None, :], jnp.exp(scores - peaks), 0.0)
            masses = lax.optimization_barrier(jnp.sum(weights, axis=2))
            probs = weights.astype(jnp.bfloat16).reshape(row_block * per_group, key_total)
            summed = jnp.dot(probs, group_values, preferred_element_type=jnp.float32).reshape(row_block, per_group, HEAD_DIM)
            return (summed / masses[:, :, None]).astype(jnp.bfloat16)
        blocks = lax.map(block_attention, jnp.arange(SPAN // row_block, dtype=jnp.int32))
        return blocks.reshape(SPAN, per_group, HEAD_DIM)
    grouped = lax.map(group_attention, jnp.arange(KV_HEADS, dtype=jnp.int32))
    attended = jnp.transpose(grouped, (1, 0, 2, 3)).reshape(SPAN, HEADS * HEAD_DIM)
    projected = jnp.dot(attended, out_weight, preferred_element_type=jnp.float32)
    mid = (residual.astype(jnp.float32) + projected).astype(jnp.bfloat16)
    mid_wide = mid.astype(jnp.float32)
    scale_rows = lax.rsqrt(lax.optimization_barrier(jnp.mean(mid_wide * mid_wide, axis=1, keepdims=True)) + EPSILON)
    normed = (mid_wide * scale_rows * norm_gain.astype(jnp.float32)).astype(jnp.bfloat16)
    logits = jnp.dot(normed, router_weight, preferred_element_type=jnp.float32)
    one_hot = expert_ids[:, :, None] == jnp.arange(EXPERTS, dtype=jnp.int32)[None, None, :]
    picked = lax.optimization_barrier(jnp.sum(jnp.where(one_hot, logits[:, None, :], 0.0), axis=2))
    gate_vals = 1.0 / (1.0 + jnp.exp(picked[:, ::-1] - picked))
    pair_hot = one_hot.reshape(SPAN * TOPK, EXPERTS).astype(jnp.int32)
    earlier_count = jnp.cumsum(pair_hot, axis=0) - pair_hot
    pair_slot = lax.optimization_barrier(jnp.sum(earlier_count * pair_hot, axis=1))
    slot_of = pair_slot.reshape(SPAN, TOPK)
    is_kept = slot_of < CAP
    pair_expert = expert_ids.reshape(-1)
    pair_token = jnp.arange(SPAN * TOPK, dtype=jnp.int32) // TOPK
    expert_sum = jnp.zeros((SPAN, D), jnp.float32)
    for expert in range(EXPERTS):
        match = (pair_expert == expert)[None, :] & (pair_slot[None, :] == jnp.arange(CAP, dtype=jnp.int32)[:, None])
        slot_token = lax.optimization_barrier(jnp.sum(jnp.where(match, pair_token[None, :], 0), axis=1)).astype(jnp.int32)
        slot_live = jnp.any(match, axis=1)
        slot_inputs = jnp.where(slot_live[:, None], normed[slot_token], jnp.zeros((), jnp.bfloat16))
        gate_part = jnp.dot(slot_inputs, gate_weight[:, expert * FF:(expert + 1) * FF], preferred_element_type=jnp.float32)
        up_part = jnp.dot(slot_inputs, up_weight[:, expert * FF:(expert + 1) * FF], preferred_element_type=jnp.float32)
        hidden = (jax.nn.silu(gate_part) * up_part).astype(jnp.bfloat16)
        expert_out = jnp.dot(hidden, down_weight[expert * FF:(expert + 1) * FF, :], preferred_element_type=jnp.float32)
        for pick_no in range(TOPK):
            in_use = (expert_ids[:, pick_no] == expert) & is_kept[:, pick_no]
            slot_idx = jnp.clip(slot_of[:, pick_no], 0, CAP - 1)
            expert_sum = expert_sum + jnp.where(in_use[:, None], gate_vals[:, pick_no][:, None] * expert_out[slot_idx], 0.0)
    return (mid.astype(jnp.float32) + expert_sum).astype(jnp.bfloat16)
```

```python
import math

import jax
import jax.numpy as jnp
from jax import lax
from jax.experimental import pallas as pl
from jax.experimental.pallas import tpu as pltpu
from jax.sharding import PartitionSpec as P

D = 6144
HEAD_DIM = 128
EXPERTS = 4
FF = 8192
TOPK = 2
SPAN = 256
CAP = 160
NZ = 8
NE = 8
FINE = 2
HEADS_LOCAL = 6
BLOCK_TOKENS = 16
BLOCK_ROWS = BLOCK_TOKENS * HEADS_LOCAL
ROWS = NZ * BLOCK_ROWS
Q_BLOCK = 256
CHUNK = 4096
MASKED_CHUNK = 1024
MESSAGE_ROWS = BLOCK_ROWS + 16
COLS = 768
HALF = 384
EPSILON = 1e-05
MASKED = -1e30
EXP2_SCALE = HEAD_DIM**-0.5 * math.log2(math.e)
BF16 = jnp.bfloat16
F32 = jnp.float32

Z_GROUPS = [[2 * z + core for z in range(NZ)] for core in range(2)]
SIBLINGS = [(c, c ^ 1) for c in range(2 * NZ)]


def exchange_z(blocks):
    return lax.all_to_all(blocks, "ctx", 0, 0, axis_index_groups=Z_GROUPS, tiled=True)


def exchange_exp(blocks):
    return lax.all_to_all(blocks, "exp", 0, 0, tiled=True)


def sibling(x):
    return lax.ppermute(x, "ctx", SIBLINGS)


VMEM = pl.BlockSpec(memory_space=pltpu.VMEM)
SMEM = pl.BlockSpec(memory_space=pltpu.SMEM)
ANY = pl.BlockSpec(memory_space=pl.ANY)


def call(kernel, shape, *args, specs=None, dtype=BF16, limit=32, flops=1 << 20, scratch=()):
    return pl.pallas_call(
        kernel,
        out_shape=jax.ShapeDtypeStruct(shape, dtype),
        in_specs=specs or [VMEM] * len(args),
        out_specs=VMEM,
        scratch_shapes=scratch,
        compiler_params=pltpu.CompilerParams(vmem_limit_bytes=limit << 20),
        cost_estimate=pl.CostEstimate(flops=flops, bytes_accessed=1 << 20, transcendentals=0),
    )(*args)


def first_message_kernel(q, residual, out):
    res = residual[...].astype(F32)
    row = lax.broadcasted_iota(jnp.int32, (16, HEAD_DIM), 0)
    for z in range(NZ):
        for h in range(HEADS_LOCAL):
            out[z, h * BLOCK_TOKENS : (h + 1) * BLOCK_TOKENS, :] = q[
                :, h * HEAD_DIM : (h + 1) * HEAD_DIM
            ]
        rows = jnp.zeros((16, HEAD_DIM), F32)
        for j in range(COLS // HEAD_DIM):
            start = z * COLS + j * HEAD_DIM
            piece = res[:, start : start + HEAD_DIM]
            for f in range(FINE):
                rows = jnp.where(row == j * FINE + f, piece[f : f + 1, :], rows)
        out[z, BLOCK_ROWS:, :] = rows.astype(BF16)


def split3(x):
    first = x.astype(BF16).astype(F32)
    rest = x - first
    second = rest.astype(BF16).astype(F32)
    return first, second, rest - second


def attention_kernel(
    info, first, k0, v0, k1, v1, sk, sv, out, q, keys, values, peak, carried, sems
):
    copies = []
    for i, (source, target) in enumerate(((k0, keys), (v0, values), (k1, keys), (v1, values))):
        place = pl.ds(i // 2 * CHUNK, CHUNK)
        copies.append(pltpu.make_async_copy(source, target.at[place, :], sems.at[i]))
        copies[i].start()
    q[...] = first[:, :BLOCK_ROWS, :].reshape(ROWS, HEAD_DIM)
    blocks = ROWS // Q_BLOCK

    def columns(b):
        return slice(b * Q_BLOCK, (b + 1) * Q_BLOCK)

    def scores_of(rows, b):
        return lax.dot_general(
            rows, q[columns(b), :], (((1,), (1,)), ((), ())), preferred_element_type=F32
        )

    def with_ones(rows):
        return jnp.concatenate([rows.T, jnp.ones((16, rows.shape[0]), BF16)], axis=0)

    core = info[2]
    span_rows = 2 * BLOCK_TOKENS
    span_values = with_ones(sv[...])
    for b in range(blocks):
        row = lax.broadcasted_iota(jnp.int32, (span_rows, Q_BLOCK), 0)
        col = lax.broadcasted_iota(jnp.int32, (span_rows, Q_BLOCK), 1) + b * Q_BLOCK
        token = col // BLOCK_ROWS * span_rows + core * BLOCK_TOKENS + col % BLOCK_TOKENS
        allowed = info[3] + row <= token
        s = jnp.where(allowed, scores_of(sk[...], b), MASKED)
        top = jnp.max(s, axis=0, keepdims=True)
        w = jnp.where(allowed, jnp.exp2((s - top) * EXP2_SCALE), 0.0).astype(BF16)
        peak[:, columns(b)] = jnp.broadcast_to(top, (8, Q_BLOCK))
        carried[:, columns(b)] = jnp.dot(span_values, w, preferred_element_type=F32)

    def soften(s, b):
        before = peak[:1, columns(b)]
        top = jnp.maximum(before, jnp.max(s, axis=0, keepdims=True))
        peak[:, columns(b)] = jnp.broadcast_to(top, (8, Q_BLOCK))
        w = jnp.exp2((s - top) * EXP2_SCALE).astype(BF16)
        return w, jnp.exp2((before - top) * EXP2_SCALE)

    def gather(b, w, factor, rows):
        carried[:, columns(b)] = carried[:, columns(b)] * factor + jnp.dot(
            rows, w, preferred_element_type=F32
        )

    for part in range(2):
        valid = info[part]
        copies[2 * part].wait()
        copies[2 * part + 1].wait()

        @pl.when(valid == CHUNK)
        def _(part=part):
            place = slice(part * CHUNK, (part + 1) * CHUNK)
            key_rows = keys[place, :]
            value_rows = with_ones(values[place, :])
            s = scores_of(key_rows, 0)
            earlier = None
            for b in range(blocks):
                later = scores_of(key_rows, b + 1) if b + 1 < blocks else None
                current = soften(s, b)
                if earlier is not None:
                    gather(b - 1, *earlier, value_rows)
                earlier, s = current, later
            gather(blocks - 1, *earlier, value_rows)

        @pl.when(valid < CHUNK)
        def _(part=part, valid=valid):
            @pl.loop(0, (valid + MASKED_CHUNK - 1) // MASKED_CHUNK)
            def _(j):
                start = pl.multiple_of(part * CHUNK + j * MASKED_CHUNK, MASKED_CHUNK)
                key_rows = keys[pl.ds(start, MASKED_CHUNK), :]
                value_rows = with_ones(values[pl.ds(start, MASKED_CHUNK), :])
                row = lax.broadcasted_iota(jnp.int32, (MASKED_CHUNK, Q_BLOCK), 0)
                for b in range(blocks):
                    s = scores_of(key_rows, b)
                    s = jnp.where(row + j * MASKED_CHUNK < valid, s, MASKED)
                    gather(b, *soften(s, b), value_rows)

    rows = carried[:HEAD_DIM, :].T.astype(BF16)
    out[:, :BLOCK_ROWS, :] = rows.reshape(NZ, BLOCK_ROWS, HEAD_DIM)
    terms = split3(peak[:1, :]) + split3(carried[HEAD_DIM : HEAD_DIM + 1, :])
    row = lax.broadcasted_iota(jnp.int32, (16, ROWS), 0)
    stats = jnp.zeros((16, ROWS), F32)
    for i, term in enumerate(terms):
        stats = jnp.where(row == i, term, stats)
    for z in range(NZ):
        turned = stats if z == 0 else pltpu.roll(stats, ROWS - z * BLOCK_ROWS, 1)
        out[z, BLOCK_ROWS:, :] = turned[:, :HEAD_DIM].astype(BF16)


def combine_kernel(message, out):
    peaks, masses = [], []
    for z in range(NZ):
        r = message[z, BLOCK_ROWS:, :].astype(F32)
        peaks.append(r[0:1] + r[1:2] + r[2:3])
        masses.append(r[3:4] + r[4:5] + r[5:6])
    top = peaks[0]
    for z in range(1, NZ):
        top = jnp.maximum(top, peaks[z])
    factors = [jnp.exp2((p - top) * EXP2_SCALE) for p in peaks]
    total = factors[0] * masses[0]
    for z in range(1, NZ):
        total = total + factors[z] * masses[z]
    row = lax.broadcasted_iota(jnp.int32, (HEAD_DIM, HEAD_DIM), 0)
    shares = jnp.zeros((HEAD_DIM, HEAD_DIM), F32)
    for z in range(NZ):
        shares = jnp.where(row == z, factors[z] / total, shares)
    shares = shares.T
    rows = jnp.zeros((BLOCK_ROWS, HEAD_DIM), F32)
    for z in range(NZ):
        rows = rows + message[z, :BLOCK_ROWS, :].astype(F32) * shares[:BLOCK_ROWS, z : z + 1]
    rows = rows.astype(BF16)
    for h in range(HEADS_LOCAL):
        piece = rows[h * BLOCK_TOKENS : (h + 1) * BLOCK_TOKENS]
        for z in range(NZ):
            out[z, :, h * HEAD_DIM : (h + 1) * HEAD_DIM] = piece


def project_kernel(info, x, own, other, out):
    r = lax.broadcasted_iota(jnp.int32, (128, 128), 0)
    c = lax.broadcasted_iota(jnp.int32, (128, 128), 1)
    wanted = r % 16 // FINE * 16 + r // 16 * FINE + r % FINE
    turn = jnp.where(c == wanted, 1.0, 0.0).astype(BF16)
    rows = jnp.dot(turn, x[...].reshape(128, COLS), preferred_element_type=F32).astype(BF16)
    core = info[2]
    for weight, side in ((own, core), (other, 1 - core)):
        part = jnp.dot(rows, weight[...], preferred_element_type=F32).astype(BF16)
        out[:, :, pl.ds(pl.multiple_of(side * HALF, HALF), HALF)] = part.reshape(NE, 16, HALF)


def mid_kernel(parts, message, out):
    total = parts[0].astype(F32)
    for e in range(1, NE):
        total = total + parts[e].astype(F32)
    rows = message[:, BLOCK_ROWS:, :].reshape(128, HEAD_DIM)
    r = lax.broadcasted_iota(jnp.int32, (16, 128), 0)
    c = lax.broadcasted_iota(jnp.int32, (16, 128), 1)
    for j in range(COLS // HEAD_DIM):
        pick = jnp.where(c == r // FINE * 16 + j * FINE + r % FINE, 1.0, 0.0).astype(BF16)
        place = slice(j * HEAD_DIM, (j + 1) * HEAD_DIM)
        res = jnp.dot(pick, rows, preferred_element_type=F32)
        mid = (res + total[:, place]).astype(BF16)
        for z in range(NZ):
            out[z, :, place] = mid


def norm_kernel(info, parts, gain, out, own):
    squares = jnp.zeros((16, 1), F32)
    for z in range(NZ):
        wide = parts[z].astype(F32)
        squares = squares + jnp.sum(wide * wide, axis=1, keepdims=True)
    scale = lax.rsqrt(squares * (1.0 / D) + EPSILON)
    r = lax.broadcasted_iota(jnp.int32, (16, 16), 0)
    c = lax.broadcasted_iota(jnp.int32, (16, 16), 1)
    pick = jnp.where((c == info[4] * FINE + r) & (r < FINE), 1.0, 0.0).astype(BF16)
    for z in range(NZ):
        place = slice(z * COLS, (z + 1) * COLS)
        mid = parts[z]
        normed = (mid.astype(F32) * scale * gain[:, place].astype(F32)).astype(BF16)
        for e in range(NE):
            out[e, :, place] = normed
        own[:, place] = jnp.dot(pick, mid, preferred_element_type=F32).astype(BF16)


MOE_STEPS = 8
MOE_TILE = D // MOE_STEPS


def moe_kernel(
    info, x, ids, router, g0, g1, u0, u1, d0, d1, out, gate, up, logits, hidden, share
):
    step = pl.program_id(0)
    units = g0.shape[1]

    @pl.when(step == 0)
    def _():
        gate[...] = jnp.zeros(gate.shape, F32)
        up[...] = jnp.zeros(up.shape, F32)
        logits[...] = jnp.zeros(logits.shape, F32)

    @pl.when(step < MOE_STEPS)
    def _():
        place = pl.ds(pl.multiple_of(step * MOE_TILE, MOE_TILE), MOE_TILE)
        rows = x[:, :, place].reshape(128, MOE_TILE)
        for i, (g, u) in enumerate(((g0, u0), (g1, u1))):
            side = slice(i * units, (i + 1) * units)
            gate[:, side] += jnp.dot(rows, g[...], preferred_element_type=F32)
            up[:, side] += jnp.dot(rows, u[...], preferred_element_type=F32)
        logits[...] += lax.dot_general(
            rows, router[:, place], (((1,), (1,)), ((), ())), preferred_element_type=F32
        )

    @pl.when(step == MOE_STEPS - 1)
    def _():
        g = gate[...]
        hidden[...] = (g / (1.0 + jnp.exp(-g)) * up[...]).astype(BF16)
        core, expert = info[2], info[5]
        r = lax.broadcasted_iota(jnp.int32, (128, SPAN), 0)
        u = lax.broadcasted_iota(jnp.int32, (128, SPAN), 1)
        token = (r % 16 // FINE * 2 + core) * BLOCK_TOKENS + r // 16 * FINE + r % FINE
        leading, trailing = ids[0:1, :], ids[1:2, :]
        chosen = (leading == expert) | (trailing == expert)
        other = jnp.where(leading == expert, trailing, leading)
        earlier = jnp.sum(jnp.where(chosen & (u < token), 1.0, 0.0), axis=1, keepdims=True)
        mine = jnp.sum(jnp.where(chosen & (u == token), 1.0, 0.0), axis=1, keepdims=True)
        other_id = jnp.sum(jnp.where(u == token, other.astype(F32), 0.0), axis=1, keepdims=True)
        lane = lax.broadcasted_iota(jnp.int32, logits.shape, 1)
        values = logits[...]
        own_logit = jnp.sum(jnp.where(lane == expert, values, 0.0), axis=1, keepdims=True)
        other_logit = jnp.sum(
            jnp.where(lane.astype(F32) == other_id, values, 0.0), axis=1, keepdims=True
        )
        active = (mine > 0.5) & (earlier < CAP - 0.5)
        share[...] = jnp.broadcast_to(
            jnp.where(active, 1.0 / (1.0 + jnp.exp(other_logit - own_logit)), 0.0), share.shape
        )

    @pl.when(step >= MOE_STEPS)
    def _():
        total = jnp.dot(hidden[:, :units], d0[...], preferred_element_type=F32)
        total = total + jnp.dot(hidden[:, units:], d1[...], preferred_element_type=F32)
        out[...] = (total * share[:, :1]).astype(BF16).reshape(NE, 16, MOE_TILE)


def experts(info, x, ids, router, g0, g1, u0, u1, d0, d1):
    units = g0.shape[1]
    wide = pl.BlockSpec((MOE_TILE, units), lambda i: (jnp.minimum(i, MOE_STEPS - 1), 0))
    down = pl.BlockSpec((units, MOE_TILE), lambda i: (0, jnp.maximum(i - MOE_STEPS, 0)))

    def whole(a):
        return pl.BlockSpec(a.shape, lambda i: (0,) * a.ndim)

    return pl.pallas_call(
        moe_kernel,
        grid=(2 * MOE_STEPS,),
        out_shape=jax.ShapeDtypeStruct((NE, 16, D), BF16),
        in_specs=[SMEM, whole(x), whole(ids), whole(router)] + [wide] * 4 + [down] * 2,
        out_specs=pl.BlockSpec(
            (NE, 16, MOE_TILE), lambda i: (0, 0, jnp.maximum(i - MOE_STEPS, 0))
        ),
        scratch_shapes=[
            pltpu.VMEM((128, 2 * units), F32),
            pltpu.VMEM((128, 2 * units), F32),
            pltpu.VMEM((128, 8), F32),
            pltpu.VMEM((128, 2 * units), BF16),
            pltpu.VMEM((128, 128), F32),
        ],
        compiler_params=pltpu.CompilerParams(vmem_limit_bytes=24 << 20),
        cost_estimate=pl.CostEstimate(
            flops=6 * 128 * D * 2 * units, bytes_accessed=22 << 20, transcendentals=128 * 512
        ),
    )(info, x, ids, router, g0, g1, u0, u1, d0, d1)


def sum_kernel(parts, out):
    total = parts[0].astype(F32)
    for e in range(1, NE):
        total = total + parts[e].astype(F32)
    for z in range(NZ):
        out[z] = total[z * FINE : (z + 1) * FINE].astype(BF16)


def last_kernel(parts, own, out):
    total = own[:, :].astype(F32)[:FINE]
    for z in range(NZ):
        total = total + parts[z].astype(F32)
    out[...] = total.astype(BF16)


def shards(
    queries,
    span_keys,
    span_values,
    cache_keys,
    cache_values,
    span_start,
    residual,
    out_weight,
    norm_gain,
    router_weight,
    expert_ids,
    gate_weight,
    up_weight,
    down_weight,
):
    ctx_index = lax.axis_index("ctx")
    core = ctx_index % 2
    z_index = ctx_index // 2
    key_rows = cache_keys.shape[0]

    other_keys = sibling(cache_keys)
    other_values = sibling(cache_values)
    span_own = jnp.concatenate([span_keys, span_values], axis=1)
    other_span = sibling(span_own)
    other_out = sibling(out_weight)
    other_gate = sibling(gate_weight)
    other_up = sibling(up_weight)
    other_down = sibling(down_weight)

    first = exchange_z(
        call(first_message_kernel, (NZ, MESSAGE_ROWS, HEAD_DIM), queries, residual)
    )

    def valid(index):
        return jnp.clip(span_start[0] - index * key_rows, 0, key_rows)

    own_first = core == 0
    span_both = jnp.concatenate(
        [jnp.where(own_first, span_own, other_span), jnp.where(own_first, other_span, span_own)], axis=0
    )
    info = jnp.stack(
        [
            valid(ctx_index),
            valid(ctx_index ^ 1),
            core,
            z_index * 2 * BLOCK_TOKENS,
            z_index,
            z_index // 2,
        ]
    ).astype(jnp.int32)
    second = exchange_z(
        call(
            attention_kernel,
            (NZ, MESSAGE_ROWS, HEAD_DIM),
            info,
            first,
            cache_keys,
            cache_values,
            other_keys,
            other_values,
            span_both[:, :HEAD_DIM],
            span_both[:, HEAD_DIM:],
            specs=[SMEM, VMEM, ANY, ANY, ANY, ANY, VMEM, VMEM],
            limit=48,
            flops=4 * ROWS * 2 * CHUNK * HEAD_DIM,
            scratch=[
                pltpu.VMEM((ROWS, HEAD_DIM), BF16),
                pltpu.VMEM((2 * CHUNK, HEAD_DIM), BF16),
                pltpu.VMEM((2 * CHUNK, HEAD_DIM), BF16),
                pltpu.VMEM((8, ROWS), F32),
                pltpu.VMEM((HEAD_DIM + 16, ROWS), F32),
                pltpu.SemaphoreType.DMA((4,)),
            ],
        )
    )
    third = exchange_z(call(combine_kernel, (NZ, BLOCK_TOKENS, COLS), second))
    fourth = exchange_exp(
        call(
            project_kernel,
            (NE, 16, COLS),
            info,
            third,
            out_weight,
            other_out,
            specs=[SMEM, VMEM, VMEM, VMEM],
        )
    )
    fifth = exchange_z(call(mid_kernel, (NZ, 16, COLS), fourth, first))
    normed, own_mid = pl.pallas_call(
        norm_kernel,
        out_shape=(
            jax.ShapeDtypeStruct((NE, 16, D), BF16),
            jax.ShapeDtypeStruct((16, D), BF16),
        ),
        in_specs=[SMEM, VMEM, VMEM],
        out_specs=(VMEM, VMEM),
        compiler_params=pltpu.CompilerParams(vmem_limit_bytes=16 << 20),
        cost_estimate=pl.CostEstimate(flops=1 << 20, bytes_accessed=2 << 20, transcendentals=0),
    )(info, fifth, norm_gain.reshape(1, D))
    tokens = exchange_exp(normed)

    ids = jnp.pad(expert_ids.T, ((0, 8 - TOPK), (0, 0)))
    router = jnp.pad(router_weight.T, ((0, 8 - EXPERTS), (0, 0)))
    result = experts(
        info,
        tokens,
        ids,
        router,
        gate_weight,
        other_gate,
        up_weight,
        other_up,
        down_weight,
        other_down,
    )
    sixth = exchange_exp(result)
    seventh = exchange_z(call(sum_kernel, (NZ, FINE, D), sixth))
    return call(last_kernel, (FINE, D), seventh, own_mid)


def solution(mesh):
    placed = (
        P(("dp", "ctx"), "exp"),
        P(("dp", "ctx"), "exp"),
        P(("dp", "ctx"), "exp"),
        P(("dp", "ctx"), "exp"),
        P(("dp", "ctx"), "exp"),
        P("dp"),
        P(("dp", "ctx", "exp"), None),
        P("exp", "ctx"),
        P(),
        P(),
        P("dp", None),
        P(None, ("ctx", "exp")),
        P(None, ("ctx", "exp")),
        P(("ctx", "exp"), None),
    )
    return jax.shard_map(
        shards, mesh=mesh, in_specs=placed, out_specs=P(("dp", "ctx", "exp"), None), check_vma=False
    )
```

```python
import math

import jax
import jax.numpy as jnp
from jax import lax
from jax.experimental import pallas as pl
from jax.experimental.pallas import tpu as pltpu
from jax.sharding import PartitionSpec as P

D = 6144
HEAD_DIM = 128
EXPERTS = 4
FF = 8192
TOPK = 2
SPAN = 256
CAP = 160
NZ = 8
NE = 8
FINE = 2
HEADS_LOCAL = 6
BLOCK_TOKENS = 16
BLOCK_ROWS = BLOCK_TOKENS * HEADS_LOCAL
ROWS = NZ * BLOCK_ROWS
Q_BLOCK = 256
CHUNK = 4096
MESSAGE_ROWS = BLOCK_ROWS + 16
COLS = 768
HALF = 384
EPSILON = 1e-05
MASKED = -1e30
EXP2_SCALE = HEAD_DIM**-0.5 * math.log2(math.e)
BF16 = jnp.bfloat16
F32 = jnp.float32

Z_GROUPS = [[2 * z + core for z in range(NZ)] for core in range(2)]
SIBLINGS = [(c, c ^ 1) for c in range(2 * NZ)]


def exchange_z(blocks):
    return lax.all_to_all(blocks, "ctx", 0, 0, axis_index_groups=Z_GROUPS, tiled=True)


def exchange_exp(blocks):
    return lax.all_to_all(blocks, "exp", 0, 0, tiled=True)


def sibling(x):
    return lax.ppermute(x, "ctx", SIBLINGS)


VMEM = pl.BlockSpec(memory_space=pltpu.VMEM)
SMEM = pl.BlockSpec(memory_space=pltpu.SMEM)
ANY = pl.BlockSpec(memory_space=pl.ANY)


def in_hbm(x):
    return pltpu.with_memory_space_constraint(x, pltpu.HBM)


def call(kernel, shape, *args, specs=None, dtype=BF16, limit=32, flops=1 << 20, scratch=()):
    return pl.pallas_call(
        kernel,
        out_shape=jax.ShapeDtypeStruct(shape, dtype),
        in_specs=specs or [VMEM] * len(args),
        out_specs=VMEM,
        scratch_shapes=scratch,
        compiler_params=pltpu.CompilerParams(vmem_limit_bytes=limit << 20),
        cost_estimate=pl.CostEstimate(flops=flops, bytes_accessed=1 << 20, transcendentals=0),
    )(*args)


def first_message_kernel(q, residual, out):
    res = residual[...].astype(F32)
    row = lax.broadcasted_iota(jnp.int32, (16, HEAD_DIM), 0)
    for z in range(NZ):
        for h in range(HEADS_LOCAL):
            out[z, h * BLOCK_TOKENS : (h + 1) * BLOCK_TOKENS, :] = q[
                :, h * HEAD_DIM : (h + 1) * HEAD_DIM
            ]
        rows = jnp.zeros((16, HEAD_DIM), F32)
        for j in range(COLS // HEAD_DIM):
            start = z * COLS + j * HEAD_DIM
            piece = res[:, start : start + HEAD_DIM]
            for f in range(FINE):
                rows = jnp.where(row == j * FINE + f, piece[f : f + 1, :], rows)
        out[z, BLOCK_ROWS:, :] = rows.astype(BF16)


def split3(x):
    first = x.astype(BF16).astype(F32)
    rest = x - first
    second = rest.astype(BF16).astype(F32)
    return first, second, rest - second


def prepare_kernel(v0, v1, k1, values, keys, sem):
    copy = pltpu.make_async_copy(k1, keys, sem)
    copy.start()
    for part, rows in enumerate((v0, v1)):
        values[part, :HEAD_DIM, :] = rows[...].T
        values[part, HEAD_DIM:, :] = jnp.ones((16, CHUNK), BF16)
    copy.wait()


def prepare(v0, v1, k1):
    return pl.pallas_call(
        prepare_kernel,
        out_shape=(
            pltpu.HBM((2, HEAD_DIM + 16, CHUNK), BF16),
            pltpu.HBM((CHUNK, HEAD_DIM), BF16),
        ),
        in_specs=[VMEM, VMEM, ANY],
        out_specs=(VMEM, ANY),
        scratch_shapes=[pltpu.SemaphoreType.DMA],
        compiler_params=pltpu.CompilerParams(vmem_limit_bytes=16 << 20),
        cost_estimate=pl.CostEstimate(flops=0, bytes_accessed=6 << 20, transcendentals=0),
    )(v0, v1, k1)


def attention_kernel(
    info, first, k0, k1, turned, sk, sv, out, q, keys, values, peak, carried, sems
):
    copies = []
    for part, source in enumerate((k0, k1)):
        copies.append(pltpu.make_async_copy(source, keys.at[part], sems.at[2 * part]))
        copies.append(
            pltpu.make_async_copy(turned.at[part], values.at[part], sems.at[2 * part + 1])
        )
    for copy in copies:
        copy.start()
    q[...] = first[:, :BLOCK_ROWS, :].reshape(ROWS, HEAD_DIM)
    blocks = ROWS // Q_BLOCK

    def columns(b):
        return slice(b * Q_BLOCK, (b + 1) * Q_BLOCK)

    def scores_of(rows, b):
        return lax.dot_general(
            rows, q[columns(b), :], (((1,), (1,)), ((), ())), preferred_element_type=F32
        )

    core = info[2]
    span_rows = 2 * BLOCK_TOKENS
    span_values = jnp.concatenate([sv[...].T, jnp.ones((16, span_rows), BF16)], axis=0)
    for b in range(blocks):
        row = lax.broadcasted_iota(jnp.int32, (span_rows, Q_BLOCK), 0)
        col = lax.broadcasted_iota(jnp.int32, (span_rows, Q_BLOCK), 1) + b * Q_BLOCK
        token = col // BLOCK_ROWS * span_rows + core * BLOCK_TOKENS + col % BLOCK_TOKENS
        allowed = info[3] + row <= token
        s = jnp.where(allowed, scores_of(sk[...], b), MASKED)
        top = jnp.max(s, axis=0, keepdims=True)
        w = jnp.where(allowed, jnp.exp2((s - top) * EXP2_SCALE), 0.0).astype(BF16)
        peak[:, columns(b)] = jnp.broadcast_to(top, (8, Q_BLOCK))
        carried[:, columns(b)] = jnp.dot(span_values, w, preferred_element_type=F32)

    def soften(s, b):
        before = peak[:1, columns(b)]
        top = jnp.maximum(before, jnp.max(s, axis=0, keepdims=True))
        peak[:, columns(b)] = jnp.broadcast_to(top, (8, Q_BLOCK))
        w = jnp.exp2((s - top) * EXP2_SCALE).astype(BF16)
        return w, jnp.exp2((before - top) * EXP2_SCALE)

    def run(parts, count, valid=None):
        items = [(part, b) for part in parts for b in range(blocks)]

        def scores(item):
            s = scores_of(keys[item[0], :count, :], item[1])
            if valid is not None:
                row = lax.broadcasted_iota(jnp.int32, (count, Q_BLOCK), 0)
                s = jnp.where(row < valid, s, MASKED)
            return s

        def gather(item, w, factor):
            part, b = item
            carried[:, columns(b)] = carried[:, columns(b)] * factor + jnp.dot(
                values[part, :, :count], w, preferred_element_type=F32
            )

        s = scores(items[0])
        earlier = None
        for i, item in enumerate(items):
            later = scores(items[i + 1]) if i + 1 < len(items) else None
            current = soften(s, item[1])
            if earlier is not None:
                gather(items[i - 1], *earlier)
            earlier, s = current, later
        gather(items[-1], *earlier)

    for copy in copies:
        copy.wait()
    everything = (info[0] == CHUNK) & (info[1] == CHUNK)

    @pl.when(everything)
    def _():
        run((0, 1), CHUNK)

    @pl.when(jnp.logical_not(everything))
    def _():
        @pl.loop(0, 2)
        def _(part):
            valid = info[part]

            @pl.when(valid == CHUNK)
            def _():
                run((part,), CHUNK)

            @pl.when((valid < CHUNK) & (valid > CHUNK // 2))
            def _():
                run((part,), CHUNK, valid)

            @pl.when((valid <= CHUNK // 2) & (valid > 0))
            def _():
                run((part,), CHUNK // 2, valid)

    rows = carried[:HEAD_DIM, :].T.astype(BF16)
    out[:, :BLOCK_ROWS, :] = rows.reshape(NZ, BLOCK_ROWS, HEAD_DIM)
    terms = split3(peak[:1, :]) + split3(carried[HEAD_DIM : HEAD_DIM + 1, :])
    row = lax.broadcasted_iota(jnp.int32, (16, ROWS), 0)
    stats = jnp.zeros((16, ROWS), F32)
    for i, term in enumerate(terms):
        stats = jnp.where(row == i, term, stats)
    for z in range(NZ):
        shifted = stats if z == 0 else pltpu.roll(stats, ROWS - z * BLOCK_ROWS, 1)
        out[z, BLOCK_ROWS:, :] = shifted[:, :HEAD_DIM].astype(BF16)


def combine_kernel(message, out):
    peaks, masses = [], []
    for z in range(NZ):
        r = message[z, BLOCK_ROWS:, :].astype(F32)
        peaks.append(r[0:1] + r[1:2] + r[2:3])
        masses.append(r[3:4] + r[4:5] + r[5:6])
    top = peaks[0]
    for z in range(1, NZ):
        top = jnp.maximum(top, peaks[z])
    factors = [jnp.exp2((p - top) * EXP2_SCALE) for p in peaks]
    total = factors[0] * masses[0]
    for z in range(1, NZ):
        total = total + factors[z] * masses[z]
    row = lax.broadcasted_iota(jnp.int32, (HEAD_DIM, HEAD_DIM), 0)
    shares = jnp.zeros((HEAD_DIM, HEAD_DIM), F32)
    for z in range(NZ):
        shares = jnp.where(row == z, factors[z] / total, shares)
    shares = shares.T
    rows = jnp.zeros((BLOCK_ROWS, HEAD_DIM), F32)
    for z in range(NZ):
        rows = rows + message[z, :BLOCK_ROWS, :].astype(F32) * shares[:BLOCK_ROWS, z : z + 1]
    rows = rows.astype(BF16)
    for h in range(HEADS_LOCAL):
        piece = rows[h * BLOCK_TOKENS : (h + 1) * BLOCK_TOKENS]
        for z in range(NZ):
            out[z, :, h * HEAD_DIM : (h + 1) * HEAD_DIM] = piece


def project_kernel(info, x, own, other, out):
    r = lax.broadcasted_iota(jnp.int32, (128, 128), 0)
    c = lax.broadcasted_iota(jnp.int32, (128, 128), 1)
    wanted = r % 16 // FINE * 16 + r // 16 * FINE + r % FINE
    turn = jnp.where(c == wanted, 1.0, 0.0).astype(BF16)
    rows = jnp.dot(turn, x[...].reshape(128, COLS), preferred_element_type=F32).astype(BF16)
    core = info[2]
    for weight, side in ((own, core), (other, 1 - core)):
        part = jnp.dot(rows, weight[...], preferred_element_type=F32).astype(BF16)
        out[:, :, pl.ds(pl.multiple_of(side * HALF, HALF), HALF)] = part.reshape(NE, 16, HALF)


def mid_kernel(parts, message, out):
    total = parts[0].astype(F32)
    for e in range(1, NE):
        total = total + parts[e].astype(F32)
    rows = message[:, BLOCK_ROWS:, :].reshape(128, HEAD_DIM)
    r = lax.broadcasted_iota(jnp.int32, (16, 128), 0)
    c = lax.broadcasted_iota(jnp.int32, (16, 128), 1)
    for j in range(COLS // HEAD_DIM):
        pick = jnp.where(c == r // FINE * 16 + j * FINE + r % FINE, 1.0, 0.0).astype(BF16)
        place = slice(j * HEAD_DIM, (j + 1) * HEAD_DIM)
        res = jnp.dot(pick, rows, preferred_element_type=F32)
        mid = (res + total[:, place]).astype(BF16)
        for z in range(NZ):
            out[z, :, place] = mid


def norm_kernel(info, parts, gain, out, own):
    squares = jnp.zeros((16, 1), F32)
    for z in range(NZ):
        wide = parts[z].astype(F32)
        squares = squares + jnp.sum(wide * wide, axis=1, keepdims=True)
    scale = lax.rsqrt(squares * (1.0 / D) + EPSILON)
    r = lax.broadcasted_iota(jnp.int32, (16, 16), 0)
    c = lax.broadcasted_iota(jnp.int32, (16, 16), 1)
    pick = jnp.where((c == info[4] * FINE + r) & (r < FINE), 1.0, 0.0).astype(BF16)
    for z in range(NZ):
        place = slice(z * COLS, (z + 1) * COLS)
        mid = parts[z]
        normed = (mid.astype(F32) * scale * gain[:, place].astype(F32)).astype(BF16)
        for e in range(NE):
            out[e, :, place] = normed
        own[:, place] = jnp.dot(pick, mid, preferred_element_type=F32).astype(BF16)


MOE_PIECES = 4
MOE_TILE = D // MOE_PIECES


def moe_kernel(info, x, ids, router, *refs):
    sources, out, held, sems = refs[:6], refs[6], refs[7:13], refs[13]
    units = sources[0].shape[1]
    copies = []
    for k in range(2 * MOE_PIECES):
        place = pl.ds(k % MOE_PIECES * MOE_TILE, MOE_TILE)
        group = range(4) if k < MOE_PIECES else range(4, 6)
        copies.append([])
        for i in group:
            at = (place, slice(None)) if i < 4 else (slice(None), place)
            copy = pltpu.make_async_copy(sources[i].at[at], held[i].at[at], sems.at[k, i % 4])
            copy.start()
            copies[k].append(copy)

    core, expert = info[2], info[5]
    rows = x[...].reshape(128, D)
    logits = lax.dot_general(
        rows, router[...], (((1,), (1,)), ((), ())), preferred_element_type=F32
    )
    r = lax.broadcasted_iota(jnp.int32, (128, SPAN), 0)
    u = lax.broadcasted_iota(jnp.int32, (128, SPAN), 1)
    token = (r % 16 // FINE * 2 + core) * BLOCK_TOKENS + r // 16 * FINE + r % FINE
    leading, trailing = ids[0:1, :], ids[1:2, :]
    chosen = (leading == expert) | (trailing == expert)
    other = jnp.where(leading == expert, trailing, leading)
    earlier = jnp.sum(jnp.where(chosen & (u < token), 1.0, 0.0), axis=1, keepdims=True)
    mine = jnp.sum(jnp.where(chosen & (u == token), 1.0, 0.0), axis=1, keepdims=True)
    other_id = jnp.sum(jnp.where(u == token, other.astype(F32), 0.0), axis=1, keepdims=True)
    lane = lax.broadcasted_iota(jnp.int32, logits.shape, 1)
    own_logit = jnp.sum(jnp.where(lane == expert, logits, 0.0), axis=1, keepdims=True)
    other_logit = jnp.sum(
        jnp.where(lane.astype(F32) == other_id, logits, 0.0), axis=1, keepdims=True
    )
    active = (mine > 0.5) & (earlier < CAP - 0.5)
    share = jnp.where(active, 1.0 / (1.0 + jnp.exp(other_logit - own_logit)), 0.0)

    sums = [jnp.zeros((128, units), F32)] * 4
    for k in range(MOE_PIECES):
        for copy in copies[k]:
            copy.wait()
        place = slice(k * MOE_TILE, (k + 1) * MOE_TILE)
        part = x[:, :, place].reshape(128, MOE_TILE)
        sums = [
            sums[i] + jnp.dot(part, held[i][place, :], preferred_element_type=F32) for i in range(4)
        ]
    hidden = [
        (sums[i] / (1.0 + jnp.exp(-sums[i])) * sums[i + 2]).astype(BF16) for i in range(2)
    ]
    for k in range(MOE_PIECES):
        for copy in copies[MOE_PIECES + k]:
            copy.wait()
        place = slice(k * MOE_TILE, (k + 1) * MOE_TILE)
        total = jnp.dot(hidden[0], held[4][:, place], preferred_element_type=F32)
        total = total + jnp.dot(hidden[1], held[5][:, place], preferred_element_type=F32)
        out[:, :, place] = (total * share).astype(BF16).reshape(NE, 16, MOE_TILE)


def experts(info, x, ids, router, *weights):
    units = weights[0].shape[1]
    return call(
        moe_kernel,
        (NE, 16, D),
        info,
        x,
        ids,
        router,
        *[in_hbm(w) for w in weights],
        specs=[SMEM] + [VMEM] * 3 + [ANY] * 6,
        limit=40,
        flops=6 * 128 * D * 512,
        scratch=[pltpu.VMEM((D, units), BF16)] * 4
        + [pltpu.VMEM((units, D), BF16)] * 2
        + [pltpu.SemaphoreType.DMA((2 * MOE_PIECES, 4))],
    )


def sum_kernel(parts, out):
    total = parts[0].astype(F32)
    for e in range(1, NE):
        total = total + parts[e].astype(F32)
    for z in range(NZ):
        out[z] = total[z * FINE : (z + 1) * FINE].astype(BF16)


def last_kernel(parts, own, out):
    total = own[:, :].astype(F32)[:FINE]
    for z in range(NZ):
        total = total + parts[z].astype(F32)
    out[...] = total.astype(BF16)


def shards(
    queries,
    span_keys,
    span_values,
    cache_keys,
    cache_values,
    span_start,
    residual,
    out_weight,
    norm_gain,
    router_weight,
    expert_ids,
    gate_weight,
    up_weight,
    down_weight,
):
    ctx_index = lax.axis_index("ctx")
    core = ctx_index % 2
    z_index = ctx_index // 2
    key_rows = cache_keys.shape[0]

    other_keys = sibling(cache_keys)
    other_values = sibling(cache_values)
    span_own = jnp.concatenate([span_keys, span_values], axis=1)
    other_span = sibling(span_own)
    other_out = sibling(out_weight)
    other_gate = sibling(gate_weight)
    other_up = sibling(up_weight)
    other_down = sibling(down_weight)

    first = exchange_z(
        call(first_message_kernel, (NZ, MESSAGE_ROWS, HEAD_DIM), in_hbm(queries), in_hbm(residual))
    )

    def valid(index):
        return jnp.clip(span_start[0] - index * key_rows, 0, key_rows)

    own_first = core == 0
    span_both = jnp.concatenate(
        [jnp.where(own_first, span_own, other_span), jnp.where(own_first, other_span, span_own)], axis=0
    )
    info = jnp.stack(
        [
            valid(ctx_index),
            valid(ctx_index ^ 1),
            core,
            z_index * 2 * BLOCK_TOKENS,
            z_index,
            z_index // 2,
        ]
    ).astype(jnp.int32)
    prepared_values, prepared_keys = prepare(in_hbm(cache_values), other_values, other_keys)
    second = exchange_z(
        call(
            attention_kernel,
            (NZ, MESSAGE_ROWS, HEAD_DIM),
            info,
            first,
            in_hbm(cache_keys),
            in_hbm(prepared_keys),
            in_hbm(prepared_values),
            span_both[:, :HEAD_DIM],
            span_both[:, HEAD_DIM:],
            specs=[SMEM, VMEM, ANY, ANY, ANY, VMEM, VMEM],
            limit=48,
            flops=4 * ROWS * 2 * CHUNK * HEAD_DIM,
            scratch=[
                pltpu.VMEM((ROWS, HEAD_DIM), BF16),
                pltpu.VMEM((2, CHUNK, HEAD_DIM), BF16),
                pltpu.VMEM((2, HEAD_DIM + 16, CHUNK), BF16),
                pltpu.VMEM((8, ROWS), F32),
                pltpu.VMEM((HEAD_DIM + 16, ROWS), F32),
                pltpu.SemaphoreType.DMA((4,)),
            ],
        )
    )
    third = exchange_z(call(combine_kernel, (NZ, BLOCK_TOKENS, COLS), second))
    fourth = exchange_exp(
        call(
            project_kernel,
            (NE, 16, COLS),
            info,
            third,
            out_weight,
            other_out,
            specs=[SMEM, VMEM, VMEM, VMEM],
        )
    )
    fifth = exchange_z(call(mid_kernel, (NZ, 16, COLS), fourth, first))
    normed, own_mid = pl.pallas_call(
        norm_kernel,
        out_shape=(
            jax.ShapeDtypeStruct((NE, 16, D), BF16),
            jax.ShapeDtypeStruct((16, D), BF16),
        ),
        in_specs=[SMEM, VMEM, VMEM],
        out_specs=(VMEM, VMEM),
        compiler_params=pltpu.CompilerParams(vmem_limit_bytes=16 << 20),
        cost_estimate=pl.CostEstimate(flops=1 << 20, bytes_accessed=2 << 20, transcendentals=0),
    )(info, fifth, in_hbm(norm_gain.reshape(1, D)))
    tokens = exchange_exp(normed)

    result = experts(
        info,
        tokens,
        in_hbm(expert_ids.T),
        in_hbm(router_weight.T),
        gate_weight,
        other_gate,
        up_weight,
        other_up,
        down_weight,
        other_down,
    )
    sixth = exchange_exp(result)
    seventh = exchange_z(call(sum_kernel, (NZ, FINE, D), sixth))
    return call(last_kernel, (FINE, D), seventh, own_mid)


def solution(mesh):
    placed = (
        P(("dp", "ctx"), "exp"),
        P(("dp", "ctx"), "exp"),
        P(("dp", "ctx"), "exp"),
        P(("dp", "ctx"), "exp"),
        P(("dp", "ctx"), "exp"),
        P("dp"),
        P(("dp", "ctx", "exp"), None),
        P("exp", "ctx"),
        P(),
        P(),
        P("dp", None),
        P(None, ("ctx", "exp")),
        P(None, ("ctx", "exp")),
        P(("ctx", "exp"), None),
    )
    return jax.shard_map(
        shards, mesh=mesh, in_specs=placed, out_specs=P(("dp", "ctx", "exp"), None), check_vma=False
    )
```

```python
import math

import jax
import jax.numpy as jnp
from jax import lax
from jax.experimental import pallas as pl
from jax.experimental.pallas import tpu as pltpu
from jax.sharding import PartitionSpec as P

D = 6144
HEAD_DIM = 128
EXPERTS = 4
FF = 8192
TOPK = 2
SPAN = 256
CAP = 160
NZ = 8
NE = 8
FINE = 2
HEADS_LOCAL = 6
BLOCK_TOKENS = 16
BLOCK_ROWS = BLOCK_TOKENS * HEADS_LOCAL
ROWS = NZ * BLOCK_ROWS
Q_BLOCK = 256
CHUNK = 4096
MESSAGE_ROWS = BLOCK_ROWS + 16
COLS = 768
HALF = 384
EPSILON = 1e-05
MASKED = -1e30
EXP2_SCALE = HEAD_DIM**-0.5 * math.log2(math.e)
BF16 = jnp.bfloat16
F32 = jnp.float32

Z_GROUPS = [[2 * z + core for z in range(NZ)] for core in range(2)]
SIBLINGS = [(c, c ^ 1) for c in range(2 * NZ)]


def exchange_z(blocks):
    return lax.all_to_all(blocks, "ctx", 0, 0, axis_index_groups=Z_GROUPS, tiled=True)


def exchange_exp(blocks):
    return lax.all_to_all(blocks, "exp", 0, 0, tiled=True)


def sibling(x):
    return lax.ppermute(x, "ctx", SIBLINGS)


VMEM = pl.BlockSpec(memory_space=pltpu.VMEM)
SMEM = pl.BlockSpec(memory_space=pltpu.SMEM)
ANY = pl.BlockSpec(memory_space=pl.ANY)


def in_hbm(x):
    return pltpu.with_memory_space_constraint(x, pltpu.HBM)


def in_vmem(x):
    return pltpu.with_memory_space_constraint(x, pltpu.VMEM)


def call(
    kernel,
    shape,
    *args,
    specs=None,
    space=jax.ShapeDtypeStruct,
    limit=32,
    flops=1 << 20,
    scratch=(),
):
    return pl.pallas_call(
        kernel,
        out_shape=space(shape, BF16),
        in_specs=specs or [VMEM] * len(args),
        out_specs=VMEM,
        scratch_shapes=scratch,
        compiler_params=pltpu.CompilerParams(vmem_limit_bytes=limit << 20),
        cost_estimate=pl.CostEstimate(flops=flops, bytes_accessed=1 << 20, transcendentals=0),
    )(*args)


def first_message_kernel(q, residual, out):
    res = residual[...].astype(F32)
    row = lax.broadcasted_iota(jnp.int32, (16, HEAD_DIM), 0)
    for z in range(NZ):
        for h in range(HEADS_LOCAL):
            out[z, h * BLOCK_TOKENS : (h + 1) * BLOCK_TOKENS, :] = q[
                :, h * HEAD_DIM : (h + 1) * HEAD_DIM
            ]
        rows = jnp.zeros((16, HEAD_DIM), F32)
        for j in range(COLS // HEAD_DIM):
            start = z * COLS + j * HEAD_DIM
            piece = res[:, start : start + HEAD_DIM]
            for f in range(FINE):
                rows = jnp.where(row == j * FINE + f, piece[f : f + 1, :], rows)
        out[z, BLOCK_ROWS:, :] = rows.astype(BF16)


def split3(x):
    first = x.astype(BF16).astype(F32)
    rest = x - first
    second = rest.astype(BF16).astype(F32)
    return first, second, rest - second


def prepare_kernel(v0, v1, k1, values, keys, sem):
    copy = pltpu.make_async_copy(k1, keys, sem)
    copy.start()
    for part, rows in enumerate((v0, v1)):
        values[part, :HEAD_DIM, :] = rows[...].T
        values[part, HEAD_DIM:, :] = jnp.ones((16, CHUNK), BF16)
    copy.wait()


def prepare(v0, v1, k1):
    return pl.pallas_call(
        prepare_kernel,
        out_shape=(
            pltpu.HBM((2, HEAD_DIM + 16, CHUNK), BF16),
            pltpu.HBM((CHUNK, HEAD_DIM), BF16),
        ),
        in_specs=[VMEM, VMEM, ANY],
        out_specs=(VMEM, ANY),
        scratch_shapes=[pltpu.SemaphoreType.DMA],
        compiler_params=pltpu.CompilerParams(vmem_limit_bytes=16 << 20),
        cost_estimate=pl.CostEstimate(flops=0, bytes_accessed=6 << 20, transcendentals=0),
    )(v0, v1, k1)


def attention_kernel(
    info, first, k0, k1, turned, sk, sv, out, q, keys, values, peak, carried, sems
):
    copies = []
    for part, source in enumerate((k0, k1)):
        copies.append(pltpu.make_async_copy(source, keys.at[part], sems.at[2 * part]))
        copies.append(
            pltpu.make_async_copy(turned.at[part], values.at[part], sems.at[2 * part + 1])
        )
    for copy in copies:
        copy.start()
    q[...] = first[:, :BLOCK_ROWS, :].reshape(ROWS, HEAD_DIM)
    blocks = ROWS // Q_BLOCK

    def columns(b):
        return slice(b * Q_BLOCK, (b + 1) * Q_BLOCK)

    def scores_of(rows, b):
        return lax.dot_general(
            rows, q[columns(b), :], (((1,), (1,)), ((), ())), preferred_element_type=F32
        )

    core = info[2]
    span_rows = 2 * BLOCK_TOKENS
    span_values = jnp.concatenate([sv[...].T, jnp.ones((16, span_rows), BF16)], axis=0)
    for b in range(blocks):
        row = lax.broadcasted_iota(jnp.int32, (span_rows, Q_BLOCK), 0)
        col = lax.broadcasted_iota(jnp.int32, (span_rows, Q_BLOCK), 1) + b * Q_BLOCK
        token = col // BLOCK_ROWS * span_rows + core * BLOCK_TOKENS + col % BLOCK_TOKENS
        allowed = info[3] + row <= token
        s = jnp.where(allowed, scores_of(sk[...], b), MASKED)
        top = jnp.max(s, axis=0, keepdims=True)
        w = jnp.where(allowed, jnp.exp2((s - top) * EXP2_SCALE), 0.0).astype(BF16)
        peak[:, columns(b)] = jnp.broadcast_to(top, (8, Q_BLOCK))
        carried[:, columns(b)] = jnp.dot(span_values, w, preferred_element_type=F32)

    def soften(s, b):
        before = peak[:1, columns(b)]
        top = jnp.maximum(before, jnp.max(s, axis=0, keepdims=True))
        peak[:, columns(b)] = jnp.broadcast_to(top, (8, Q_BLOCK))
        w = jnp.exp2((s - top) * EXP2_SCALE).astype(BF16)
        return w, jnp.exp2((before - top) * EXP2_SCALE)

    def run(parts, count, valid=None):
        items = [(part, b) for part in parts for b in range(blocks)]

        def scores(item):
            s = scores_of(keys[item[0], :count, :], item[1])
            if valid is not None:
                row = lax.broadcasted_iota(jnp.int32, (count, Q_BLOCK), 0)
                s = jnp.where(row < valid, s, MASKED)
            return s

        def gather(item, w, factor):
            part, b = item
            carried[:, columns(b)] = carried[:, columns(b)] * factor + jnp.dot(
                values[part, :, :count], w, preferred_element_type=F32
            )

        s = scores(items[0])
        earlier = None
        for i, item in enumerate(items):
            later = scores(items[i + 1]) if i + 1 < len(items) else None
            current = soften(s, item[1])
            if earlier is not None:
                gather(items[i - 1], *earlier)
            earlier, s = current, later
        gather(items[-1], *earlier)

    for copy in copies:
        copy.wait()
    everything = (info[0] == CHUNK) & (info[1] == CHUNK)

    @pl.when(everything)
    def _():
        run((0, 1), CHUNK)

    @pl.when(jnp.logical_not(everything))
    def _():
        @pl.loop(0, 2)
        def _(part):
            valid = info[part]

            @pl.when(valid == CHUNK)
            def _():
                run((part,), CHUNK)

            @pl.when((valid < CHUNK) & (valid > CHUNK // 2))
            def _():
                run((part,), CHUNK, valid)

            @pl.when((valid <= CHUNK // 2) & (valid > 0))
            def _():
                run((part,), CHUNK // 2, valid)

    rows = carried[:HEAD_DIM, :].T.astype(BF16)
    out[:, :BLOCK_ROWS, :] = rows.reshape(NZ, BLOCK_ROWS, HEAD_DIM)
    terms = split3(peak[:1, :]) + split3(carried[HEAD_DIM : HEAD_DIM + 1, :])
    row = lax.broadcasted_iota(jnp.int32, (16, ROWS), 0)
    stats = jnp.zeros((16, ROWS), F32)
    for i, term in enumerate(terms):
        stats = jnp.where(row == i, term, stats)
    for z in range(NZ):
        shifted = stats if z == 0 else pltpu.roll(stats, ROWS - z * BLOCK_ROWS, 1)
        out[z, BLOCK_ROWS:, :] = shifted[:, :HEAD_DIM].astype(BF16)


def combine_kernel(message, *refs):
    out = refs[len(refs) // 2]
    peaks, masses = [], []
    for z in range(NZ):
        r = message[z, BLOCK_ROWS:, :].astype(F32)
        peaks.append(r[0:1] + r[1:2] + r[2:3])
        masses.append(r[3:4] + r[4:5] + r[5:6])
    top = peaks[0]
    for z in range(1, NZ):
        top = jnp.maximum(top, peaks[z])
    factors = [jnp.exp2((p - top) * EXP2_SCALE) for p in peaks]
    total = factors[0] * masses[0]
    for z in range(1, NZ):
        total = total + factors[z] * masses[z]
    row = lax.broadcasted_iota(jnp.int32, (HEAD_DIM, HEAD_DIM), 0)
    shares = jnp.zeros((HEAD_DIM, HEAD_DIM), F32)
    for z in range(NZ):
        shares = jnp.where(row == z, factors[z] / total, shares)
    shares = shares.T
    rows = jnp.zeros((BLOCK_ROWS, HEAD_DIM), F32)
    for z in range(NZ):
        rows = rows + message[z, :BLOCK_ROWS, :].astype(F32) * shares[:BLOCK_ROWS, z : z + 1]
    rows = rows.astype(BF16)
    for h in range(HEADS_LOCAL):
        piece = rows[h * BLOCK_TOKENS : (h + 1) * BLOCK_TOKENS]
        for z in range(NZ):
            out[z, :, h * HEAD_DIM : (h + 1) * HEAD_DIM] = piece


def call_and_pass(kernel, shape, args, carried):
    count, first = len(carried), len(args)
    return pl.pallas_call(
        kernel,
        out_shape=[jax.ShapeDtypeStruct(shape, BF16)]
        + [jax.ShapeDtypeStruct(c.shape, c.dtype) for c in carried],
        in_specs=[VMEM] * first + [ANY] * count,
        out_specs=[VMEM] + [ANY] * count,
        input_output_aliases={first + i: 1 + i for i in range(count)},
        compiler_params=pltpu.CompilerParams(vmem_limit_bytes=16 << 20),
        cost_estimate=pl.CostEstimate(flops=1 << 20, bytes_accessed=1 << 20, transcendentals=0),
    )(*args, *carried)


def project_kernel(info, x, own, other, out):
    r = lax.broadcasted_iota(jnp.int32, (128, 128), 0)
    c = lax.broadcasted_iota(jnp.int32, (128, 128), 1)
    wanted = r % 16 // FINE * 16 + r // 16 * FINE + r % FINE
    turn = jnp.where(c == wanted, 1.0, 0.0).astype(BF16)
    rows = jnp.dot(turn, x[...].reshape(128, COLS), preferred_element_type=F32).astype(BF16)
    core = info[2]
    for weight, side in ((own, core), (other, 1 - core)):
        part = jnp.dot(rows, weight[...], preferred_element_type=F32).astype(BF16)
        out[:, :, pl.ds(pl.multiple_of(side * HALF, HALF), HALF)] = part.reshape(NE, 16, HALF)


def mid_kernel(parts, message, out):
    total = parts[0].astype(F32)
    for e in range(1, NE):
        total = total + parts[e].astype(F32)
    rows = message[:, BLOCK_ROWS:, :].reshape(128, HEAD_DIM)
    r = lax.broadcasted_iota(jnp.int32, (16, 128), 0)
    c = lax.broadcasted_iota(jnp.int32, (16, 128), 1)
    for j in range(COLS // HEAD_DIM):
        pick = jnp.where(c == r // FINE * 16 + j * FINE + r % FINE, 1.0, 0.0).astype(BF16)
        place = slice(j * HEAD_DIM, (j + 1) * HEAD_DIM)
        res = jnp.dot(pick, rows, preferred_element_type=F32)
        mid = (res + total[:, place]).astype(BF16)
        for z in range(NZ):
            out[z, :, place] = mid


def norm_kernel(info, parts, gain, *refs):
    out, own = refs[len(refs) // 2 - 1 : len(refs) // 2 + 1]
    squares = jnp.zeros((16, 1), F32)
    for z in range(NZ):
        wide = parts[z].astype(F32)
        squares = squares + jnp.sum(wide * wide, axis=1, keepdims=True)
    scale = lax.rsqrt(squares * (1.0 / D) + EPSILON)
    r = lax.broadcasted_iota(jnp.int32, (16, 16), 0)
    c = lax.broadcasted_iota(jnp.int32, (16, 16), 1)
    pick = jnp.where((c == info[4] * FINE + r) & (r < FINE), 1.0, 0.0).astype(BF16)
    for z in range(NZ):
        place = slice(z * COLS, (z + 1) * COLS)
        mid = parts[z]
        normed = (mid.astype(F32) * scale * gain[:, place].astype(F32)).astype(BF16)
        for e in range(NE):
            out[e, :, place] = normed
        own[:, place] = jnp.dot(pick, mid, preferred_element_type=F32).astype(BF16)


MOE_PIECES = 4
MOE_TILE = D // MOE_PIECES


def moe_kernel(info, x, ids_source, router_source, *refs):
    sources, out, held, sems = refs[:6], refs[6], refs[7:13], refs[13]
    ids, router, small_sems = refs[14:]
    units = sources[0].shape[1]
    small = (
        pltpu.make_async_copy(ids_source, ids, small_sems.at[0]),
        pltpu.make_async_copy(router_source, router, small_sems.at[1]),
    )
    for copy in small:
        copy.start()
    copies = []
    for k in range(2 * MOE_PIECES):
        place = pl.ds(k % MOE_PIECES * MOE_TILE, MOE_TILE)
        group = range(4) if k < MOE_PIECES else range(4, 6)
        copies.append([])
        for i in group:
            at = (place, slice(None)) if i < 4 else (slice(None), place)
            copy = pltpu.make_async_copy(sources[i].at[at], held[i].at[at], sems.at[k, i % 4])
            copy.start()
            copies[k].append(copy)

    sums = [jnp.zeros((128, units), F32)] * 4
    for k in range(MOE_PIECES):
        for copy in copies[k]:
            copy.wait()
        place = slice(k * MOE_TILE, (k + 1) * MOE_TILE)
        part = x[:, :, place].reshape(128, MOE_TILE)
        sums = [
            sums[i] + jnp.dot(part, held[i][place, :], preferred_element_type=F32) for i in range(4)
        ]
    hidden = [
        (sums[i] / (1.0 + jnp.exp(-sums[i])) * sums[i + 2]).astype(BF16) for i in range(2)
    ]
    for copy in small:
        copy.wait()
    core, expert = info[2], info[5]
    rows = x[...].reshape(128, D)
    logits = lax.dot_general(
        rows, router[...], (((1,), (1,)), ((), ())), preferred_element_type=F32
    )
    r = lax.broadcasted_iota(jnp.int32, (128, SPAN), 0)
    u = lax.broadcasted_iota(jnp.int32, (128, SPAN), 1)
    token = (r % 16 // FINE * 2 + core) * BLOCK_TOKENS + r // 16 * FINE + r % FINE
    leading, trailing = ids[0:1, :], ids[1:2, :]
    chosen = (leading == expert) | (trailing == expert)
    other = jnp.where(leading == expert, trailing, leading)
    earlier = jnp.sum(jnp.where(chosen & (u < token), 1.0, 0.0), axis=1, keepdims=True)
    mine = jnp.sum(jnp.where(chosen & (u == token), 1.0, 0.0), axis=1, keepdims=True)
    other_id = jnp.sum(jnp.where(u == token, other.astype(F32), 0.0), axis=1, keepdims=True)
    lane = lax.broadcasted_iota(jnp.int32, logits.shape, 1)
    own_logit = jnp.sum(jnp.where(lane == expert, logits, 0.0), axis=1, keepdims=True)
    other_logit = jnp.sum(
        jnp.where(lane.astype(F32) == other_id, logits, 0.0), axis=1, keepdims=True
    )
    active = (mine > 0.5) & (earlier < CAP - 0.5)
    share = jnp.where(active, 1.0 / (1.0 + jnp.exp(other_logit - own_logit)), 0.0)

    for k in range(MOE_PIECES):
        for copy in copies[MOE_PIECES + k]:
            copy.wait()
        place = slice(k * MOE_TILE, (k + 1) * MOE_TILE)
        total = jnp.dot(hidden[0], held[4][:, place], preferred_element_type=F32)
        total = total + jnp.dot(hidden[1], held[5][:, place], preferred_element_type=F32)
        out[:, :, place] = (total * share).astype(BF16).reshape(NE, 16, MOE_TILE)


def experts(info, x, ids, router, *weights):
    units = weights[0].shape[1]
    return call(
        moe_kernel,
        (NE, 16, D),
        info,
        x,
        ids,
        router,
        *[in_hbm(w) for w in weights],
        specs=[SMEM, VMEM] + [ANY] * 8,
        limit=40,
        flops=6 * 128 * D * 512,
        scratch=[pltpu.VMEM((D, units), BF16)] * 4
        + [pltpu.VMEM((units, D), BF16)] * 2
        + [pltpu.SemaphoreType.DMA((2 * MOE_PIECES, 4))]
        + [pltpu.VMEM(ids.shape, ids.dtype), pltpu.VMEM(router.shape, router.dtype)]
        + [pltpu.SemaphoreType.DMA((2,))],
    )


def sum_kernel(parts, out):
    total = parts[0].astype(F32)
    for e in range(1, NE):
        total = total + parts[e].astype(F32)
    for z in range(NZ):
        out[z] = total[z * FINE : (z + 1) * FINE].astype(BF16)


def last_kernel(parts, own, out):
    total = own[:, :].astype(F32)[:FINE]
    for z in range(NZ):
        total = total + parts[z].astype(F32)
    out[...] = total.astype(BF16)


def shards(
    queries,
    span_keys,
    span_values,
    cache_keys,
    cache_values,
    span_start,
    residual,
    out_weight,
    norm_gain,
    router_weight,
    expert_ids,
    gate_weight,
    up_weight,
    down_weight,
):
    ctx_index = lax.axis_index("ctx")
    core = ctx_index % 2
    z_index = ctx_index // 2
    key_rows = cache_keys.shape[0]

    other_keys = sibling(cache_keys)
    other_values = sibling(cache_values)
    span_own = jnp.concatenate([span_keys, span_values], axis=1)
    other_span = sibling(span_own)
    message = call(
        first_message_kernel,
        (NZ, MESSAGE_ROWS, HEAD_DIM),
        in_hbm(queries),
        in_hbm(residual),
        space=pltpu.HBM,
    )
    first = exchange_z(message)
    other_out = sibling(out_weight)
    other_gate = sibling(gate_weight)
    other_up = sibling(up_weight)
    other_down = sibling(down_weight)

    def valid(index):
        return jnp.clip(span_start[0] - index * key_rows, 0, key_rows)

    own_first = core == 0
    span_both = jnp.concatenate(
        [jnp.where(own_first, span_own, other_span), jnp.where(own_first, other_span, span_own)], axis=0
    )
    info = jnp.stack(
        [
            valid(ctx_index),
            valid(ctx_index ^ 1),
            core,
            z_index * 2 * BLOCK_TOKENS,
            z_index,
            z_index // 2,
        ]
    ).astype(jnp.int32)
    prepared_values, prepared_keys = prepare(in_hbm(cache_values), other_values, other_keys)
    partial = call(
        attention_kernel,
        (NZ, MESSAGE_ROWS, HEAD_DIM),
        info,
        first,
        in_hbm(cache_keys),
        in_hbm(prepared_keys),
        in_hbm(prepared_values),
        span_both[:, :HEAD_DIM],
        span_both[:, HEAD_DIM:],
        specs=[SMEM, VMEM, ANY, ANY, ANY, VMEM, VMEM],
        space=pltpu.HBM,
        limit=48,
        flops=64 * ROWS * 2 * CHUNK * HEAD_DIM,
        scratch=[
            pltpu.VMEM((ROWS, HEAD_DIM), BF16),
            pltpu.VMEM((2, CHUNK, HEAD_DIM), BF16),
            pltpu.VMEM((2, HEAD_DIM + 16, CHUNK), BF16),
            pltpu.VMEM((8, ROWS), F32),
            pltpu.VMEM((HEAD_DIM + 16, ROWS), F32),
            pltpu.SemaphoreType.DMA((4,)),
        ],
    )
    second = exchange_z(partial)
    attended, other_out, gain = call_and_pass(
        combine_kernel,
        (NZ, BLOCK_TOKENS, COLS),
        (second,),
        (in_vmem(other_out), in_hbm(norm_gain.reshape(1, D))),
    )
    third = exchange_z(attended)
    fourth = exchange_exp(
        call(
            project_kernel,
            (NE, 16, COLS),
            info,
            third,
            out_weight,
            other_out,
            specs=[SMEM, VMEM, VMEM, VMEM],
        )
    )
    fifth = exchange_z(call(mid_kernel, (NZ, 16, COLS), fourth, first))
    passed = [in_hbm(w) for w in (other_gate, other_up, other_down)]
    normed, own_mid, other_gate, other_up, other_down = pl.pallas_call(
        norm_kernel,
        out_shape=[
            jax.ShapeDtypeStruct((NE, 16, D), BF16),
            jax.ShapeDtypeStruct((16, D), BF16),
        ]
        + [jax.ShapeDtypeStruct(w.shape, w.dtype) for w in passed],
        in_specs=[SMEM, VMEM, VMEM, ANY, ANY, ANY],
        out_specs=[VMEM, VMEM, ANY, ANY, ANY],
        input_output_aliases={3: 2, 4: 3, 5: 4},
        compiler_params=pltpu.CompilerParams(vmem_limit_bytes=16 << 20),
        cost_estimate=pl.CostEstimate(flops=1 << 20, bytes_accessed=2 << 20, transcendentals=0),
    )(info, fifth, gain, *passed)
    tokens = exchange_exp(normed)

    result = experts(
        info,
        tokens,
        in_hbm(expert_ids.T),
        in_hbm(router_weight.T),
        gate_weight,
        other_gate,
        up_weight,
        other_up,
        down_weight,
        other_down,
    )
    sixth = exchange_exp(result)
    seventh = exchange_z(call(sum_kernel, (NZ, FINE, D), sixth))
    return call(last_kernel, (FINE, D), seventh, own_mid)


def solution(mesh):
    placed = (
        P(("dp", "ctx"), "exp"),
        P(("dp", "ctx"), "exp"),
        P(("dp", "ctx"), "exp"),
        P(("dp", "ctx"), "exp"),
        P(("dp", "ctx"), "exp"),
        P("dp"),
        P(("dp", "ctx", "exp"), None),
        P("exp", "ctx"),
        P(),
        P(),
        P("dp", None),
        P(None, ("ctx", "exp")),
        P(None, ("ctx", "exp")),
        P(("ctx", "exp"), None),
    )
    return jax.shard_map(
        shards, mesh=mesh, in_specs=placed, out_specs=P(("dp", "ctx", "exp"), None), check_vma=False
    )
```

```python
import math

import jax
import jax.numpy as jnp
from jax import lax
from jax.experimental import pallas as pl
from jax.experimental.pallas import tpu as pltpu
from jax.sharding import PartitionSpec as P

D = 6144
HEAD_DIM = 128
EXPERTS = 4
FF = 8192
TOPK = 2
SPAN = 256
CAP = 160
NZ = 8
NE = 8
FINE = 2
HEADS_LOCAL = 6
BLOCK_TOKENS = 16
BLOCK_ROWS = BLOCK_TOKENS * HEADS_LOCAL
ROWS = NZ * BLOCK_ROWS
Q_BLOCK = 256
CHUNK = 4096
NEAR = 256
FAR = 2.0**64
MESSAGE_ROWS = BLOCK_ROWS + 16
COLS = 768
HALF = 384
EPSILON = 1e-05
MASKED = -1e30
EXP2_SCALE = HEAD_DIM**-0.5 * math.log2(math.e)
BF16 = jnp.bfloat16
F32 = jnp.float32

Z_GROUPS = [[2 * z + core for z in range(NZ)] for core in range(2)]
SIBLINGS = [(c, c ^ 1) for c in range(2 * NZ)]


def exchange_z(blocks):
    return lax.all_to_all(blocks, "ctx", 0, 0, axis_index_groups=Z_GROUPS, tiled=True)


def exchange_exp(blocks):
    return lax.all_to_all(blocks, "exp", 0, 0, tiled=True)


def sibling(x):
    return lax.ppermute(x, "ctx", SIBLINGS)


VMEM = pl.BlockSpec(memory_space=pltpu.VMEM)
SMEM = pl.BlockSpec(memory_space=pltpu.SMEM)
ANY = pl.BlockSpec(memory_space=pl.ANY)


def in_hbm(x):
    return pltpu.with_memory_space_constraint(x, pltpu.HBM)


def in_vmem(x):
    return pltpu.with_memory_space_constraint(x, pltpu.VMEM)


def call(
    kernel,
    shape,
    *args,
    specs=None,
    space=jax.ShapeDtypeStruct,
    limit=32,
    flops=1 << 20,
    scratch=(),
):
    return pl.pallas_call(
        kernel,
        out_shape=space(shape, BF16),
        in_specs=specs or [VMEM] * len(args),
        out_specs=VMEM,
        scratch_shapes=scratch,
        compiler_params=pltpu.CompilerParams(vmem_limit_bytes=limit << 20),
        cost_estimate=pl.CostEstimate(flops=flops, bytes_accessed=1 << 20, transcendentals=0),
    )(*args)


def first_message_kernel(q, residual, out):
    res = residual[...].astype(F32)
    row = lax.broadcasted_iota(jnp.int32, (16, HEAD_DIM), 0)
    for z in range(NZ):
        for h in range(HEADS_LOCAL):
            out[z, h * BLOCK_TOKENS : (h + 1) * BLOCK_TOKENS, :] = q[
                :, h * HEAD_DIM : (h + 1) * HEAD_DIM
            ]
        rows = jnp.zeros((16, HEAD_DIM), F32)
        for j in range(COLS // HEAD_DIM):
            start = z * COLS + j * HEAD_DIM
            piece = res[:, start : start + HEAD_DIM]
            for f in range(FINE):
                rows = jnp.where(row == j * FINE + f, piece[f : f + 1, :], rows)
        out[z, BLOCK_ROWS:, :] = rows.astype(BF16)


def split3(x):
    first = x.astype(BF16).astype(F32)
    rest = x - first
    second = rest.astype(BF16).astype(F32)
    return first, second, rest - second


def prepare_kernel(v0, v1, k1, values, keys, sem):
    copy = pltpu.make_async_copy(k1, keys, sem)
    copy.start()
    for part, rows in enumerate((v0, v1)):
        values[part, :HEAD_DIM, :] = rows[...].T
        values[part, HEAD_DIM:, :] = jnp.ones((16, CHUNK), BF16)
    copy.wait()


def prepare(v0, v1, k1):
    return pl.pallas_call(
        prepare_kernel,
        out_shape=(
            pltpu.HBM((2, HEAD_DIM + 16, CHUNK), BF16),
            pltpu.HBM((CHUNK, HEAD_DIM), BF16),
        ),
        in_specs=[VMEM, VMEM, ANY],
        out_specs=(VMEM, ANY),
        scratch_shapes=[pltpu.SemaphoreType.DMA],
        compiler_params=pltpu.CompilerParams(vmem_limit_bytes=16 << 20),
        cost_estimate=pl.CostEstimate(flops=0, bytes_accessed=6 << 20, transcendentals=0),
    )(v0, v1, k1)


def attention_kernel(
    info, first, k0, k1, turned, sk, sv, out, q, keys, values, peak, carried, sems, again
):
    copies = []
    for part, source in enumerate((k0, k1)):
        copies.append(pltpu.make_async_copy(source, keys.at[part], sems.at[2 * part]))
        copies.append(
            pltpu.make_async_copy(turned.at[part], values.at[part], sems.at[2 * part + 1])
        )
    for copy in copies:
        copy.start()
    q[...] = first[:, :BLOCK_ROWS, :].reshape(ROWS, HEAD_DIM)
    blocks = ROWS // Q_BLOCK

    def columns(b):
        return slice(b * Q_BLOCK, (b + 1) * Q_BLOCK)

    def scores_of(rows, b):
        return lax.dot_general(
            rows, q[columns(b), :], (((1,), (1,)), ((), ())), preferred_element_type=F32
        )

    core = info[2]
    span_rows = 2 * BLOCK_TOKENS

    def begin():
        span_values = jnp.concatenate([sv[...].T, jnp.ones((16, span_rows), BF16)], axis=0)
        for b in range(blocks):
            row = lax.broadcasted_iota(jnp.int32, (span_rows, Q_BLOCK), 0)
            col = lax.broadcasted_iota(jnp.int32, (span_rows, Q_BLOCK), 1) + b * Q_BLOCK
            token = col // BLOCK_ROWS * span_rows + core * BLOCK_TOKENS + col % BLOCK_TOKENS
            allowed = info[3] + row <= token
            s = jnp.where(allowed, scores_of(sk[...], b), MASKED)
            top = jnp.max(s, axis=0, keepdims=True)
            w = jnp.where(allowed, jnp.exp2((s - top) * EXP2_SCALE), 0.0).astype(BF16)
            peak[:, columns(b)] = jnp.broadcast_to(top, (8, Q_BLOCK))
            carried[:, columns(b)] = jnp.dot(span_values, w, preferred_element_type=F32)

    def soften(s, b):
        before = peak[:1, columns(b)]
        top = jnp.maximum(before, jnp.max(s, axis=0, keepdims=True))
        peak[:, columns(b)] = jnp.broadcast_to(top, (8, Q_BLOCK))
        w = jnp.exp2((s - top) * EXP2_SCALE).astype(BF16)
        return w, jnp.exp2((before - top) * EXP2_SCALE)

    def soften_near(s, b, part):
        before = top = peak[:1, columns(b)]
        factor = None
        if part == 0:
            top = jnp.maximum(before, jnp.max(s[:NEAR], axis=0, keepdims=True))
            peak[:, columns(b)] = jnp.broadcast_to(top, (8, Q_BLOCK))
            factor = jnp.exp2((before - top) * EXP2_SCALE)
        return jnp.exp2((s - top) * EXP2_SCALE).astype(BF16), factor

    def run(parts, count, valid=None, near=False, wait=lambda i: None):
        items = [(part, b) for part in parts for b in range(blocks)]

        def scores(item):
            s = scores_of(keys[item[0], :count, :], item[1])
            if valid is not None:
                row = lax.broadcasted_iota(jnp.int32, (count, Q_BLOCK), 0)
                s = jnp.where(row < valid, s, MASKED)
            return s

        def gather(item, w, factor):
            part, b = item
            sums = jnp.dot(values[part, :, :count], w, preferred_element_type=F32)
            held = carried[:, columns(b)]
            carried[:, columns(b)] = (held if factor is None else held * factor) + sums

        wait(0)
        s = scores(items[0])
        wait(1)
        earlier = None
        for i, item in enumerate(items):
            later = scores(items[i + 1]) if i + 1 < len(items) else None
            current = soften_near(s, item[1], item[0]) if near else soften(s, item[1])
            if earlier is not None:
                gather(items[i - 1], *earlier)
            earlier, s = current, later
        gather(items[-1], *earlier)

    def wait_for(stage):
        for copy in copies[:1] if stage == 0 else copies[1:]:
            copy.wait()

    begin()
    everything = (info[0] == CHUNK) & (info[1] == CHUNK)
    again[0] = jnp.int32(1)

    @pl.when(everything)
    def _():
        run((0, 1), CHUNK, near=True, wait=wait_for)
        mass = carried[HEAD_DIM : HEAD_DIM + 1, :]
        far = jnp.max(jnp.where(mass < FAR, 0.0, 1.0))
        again[0] = (far > 0.5).astype(jnp.int32)

        @pl.when(again[0] == 1)
        def _():
            begin()

    @pl.when(jnp.logical_not(everything))
    def _():
        wait_for(0)
        wait_for(1)

    @pl.when(again[0] == 1)
    def _():
        @pl.loop(0, 2)
        def _(part):
            valid = info[part]

            @pl.when(valid == CHUNK)
            def _():
                run((part,), CHUNK)

            @pl.when((valid < CHUNK) & (valid > CHUNK // 2))
            def _():
                run((part,), CHUNK, valid)

            @pl.when((valid <= CHUNK // 2) & (valid > 0))
            def _():
                run((part,), CHUNK // 2, valid)

    rows = carried[:HEAD_DIM, :].T.astype(BF16)
    out[:, :BLOCK_ROWS, :] = rows.reshape(NZ, BLOCK_ROWS, HEAD_DIM)
    terms = split3(peak[:1, :]) + split3(carried[HEAD_DIM : HEAD_DIM + 1, :])
    row = lax.broadcasted_iota(jnp.int32, (16, ROWS), 0)
    stats = jnp.zeros((16, ROWS), F32)
    for i, term in enumerate(terms):
        stats = jnp.where(row == i, term, stats)
    for z in range(NZ):
        shifted = stats if z == 0 else pltpu.roll(stats, ROWS - z * BLOCK_ROWS, 1)
        out[z, BLOCK_ROWS:, :] = shifted[:, :HEAD_DIM].astype(BF16)


def combine_kernel(message, *refs):
    out = refs[len(refs) // 2]
    peaks, masses = [], []
    for z in range(NZ):
        r = message[z, BLOCK_ROWS:, :].astype(F32)
        peaks.append(r[0:1] + r[1:2] + r[2:3])
        masses.append(r[3:4] + r[4:5] + r[5:6])
    top = peaks[0]
    for z in range(1, NZ):
        top = jnp.maximum(top, peaks[z])
    factors = [jnp.exp2((p - top) * EXP2_SCALE) for p in peaks]
    total = factors[0] * masses[0]
    for z in range(1, NZ):
        total = total + factors[z] * masses[z]
    row = lax.broadcasted_iota(jnp.int32, (HEAD_DIM, HEAD_DIM), 0)
    shares = jnp.zeros((HEAD_DIM, HEAD_DIM), F32)
    for z in range(NZ):
        shares = jnp.where(row == z, factors[z] / total, shares)
    shares = shares.T
    rows = jnp.zeros((BLOCK_ROWS, HEAD_DIM), F32)
    for z in range(NZ):
        rows = rows + message[z, :BLOCK_ROWS, :].astype(F32) * shares[:BLOCK_ROWS, z : z + 1]
    rows = rows.astype(BF16)
    for h in range(HEADS_LOCAL):
        piece = rows[h * BLOCK_TOKENS : (h + 1) * BLOCK_TOKENS]
        for z in range(NZ):
            out[z, :, h * HEAD_DIM : (h + 1) * HEAD_DIM] = piece


def call_and_pass(kernel, shape, args, carried):
    count, first = len(carried), len(args)
    return pl.pallas_call(
        kernel,
        out_shape=[jax.ShapeDtypeStruct(shape, BF16)]
        + [jax.ShapeDtypeStruct(c.shape, c.dtype) for c in carried],
        in_specs=[VMEM] * first + [ANY] * count,
        out_specs=[VMEM] + [ANY] * count,
        input_output_aliases={first + i: 1 + i for i in range(count)},
        compiler_params=pltpu.CompilerParams(vmem_limit_bytes=16 << 20),
        cost_estimate=pl.CostEstimate(flops=1 << 20, bytes_accessed=1 << 20, transcendentals=0),
    )(*args, *carried)


def project_kernel(info, x, own, other, out):
    r = lax.broadcasted_iota(jnp.int32, (128, 128), 0)
    c = lax.broadcasted_iota(jnp.int32, (128, 128), 1)
    wanted = r % 16 // FINE * 16 + r // 16 * FINE + r % FINE
    turn = jnp.where(c == wanted, 1.0, 0.0).astype(BF16)
    rows = jnp.dot(turn, x[...].reshape(128, COLS), preferred_element_type=F32).astype(BF16)
    core = info[2]
    for weight, side in ((own, core), (other, 1 - core)):
        part = jnp.dot(rows, weight[...], preferred_element_type=F32).astype(BF16)
        out[:, :, pl.ds(pl.multiple_of(side * HALF, HALF), HALF)] = part.reshape(NE, 16, HALF)


def mid_kernel(parts, message, out):
    total = parts[0].astype(F32)
    for e in range(1, NE):
        total = total + parts[e].astype(F32)
    rows = message[:, BLOCK_ROWS:, :].reshape(128, HEAD_DIM)
    r = lax.broadcasted_iota(jnp.int32, (16, 128), 0)
    c = lax.broadcasted_iota(jnp.int32, (16, 128), 1)
    for j in range(COLS // HEAD_DIM):
        pick = jnp.where(c == r // FINE * 16 + j * FINE + r % FINE, 1.0, 0.0).astype(BF16)
        place = slice(j * HEAD_DIM, (j + 1) * HEAD_DIM)
        res = jnp.dot(pick, rows, preferred_element_type=F32)
        mid = (res + total[:, place]).astype(BF16)
        for z in range(NZ):
            out[z, :, place] = mid


def norm_kernel(info, parts, gain, *refs):
    out, own = refs[len(refs) // 2 - 1 : len(refs) // 2 + 1]
    squares = jnp.zeros((16, 1), F32)
    for z in range(NZ):
        wide = parts[z].astype(F32)
        squares = squares + jnp.sum(wide * wide, axis=1, keepdims=True)
    scale = lax.rsqrt(squares * (1.0 / D) + EPSILON)
    r = lax.broadcasted_iota(jnp.int32, (16, 16), 0)
    c = lax.broadcasted_iota(jnp.int32, (16, 16), 1)
    pick = jnp.where((c == info[4] * FINE + r) & (r < FINE), 1.0, 0.0).astype(BF16)
    for z in range(NZ):
        place = slice(z * COLS, (z + 1) * COLS)
        mid = parts[z]
        normed = (mid.astype(F32) * scale * gain[:, place].astype(F32)).astype(BF16)
        for e in range(NE):
            out[e, :, place] = normed
        own[:, place] = jnp.dot(pick, mid, preferred_element_type=F32).astype(BF16)


MOE_PIECES = 4
MOE_TILE = D // MOE_PIECES


def moe_kernel(info, x, ids, router, *refs):
    sources, out, held, sems = refs[:6], refs[6], refs[7:13], refs[13]
    units = sources[0].shape[1]
    copies = []
    for k in range(2 * MOE_PIECES):
        place = pl.ds(k % MOE_PIECES * MOE_TILE, MOE_TILE)
        group = range(4) if k < MOE_PIECES else range(4, 6)
        copies.append([])
        for i in group:
            at = (place, slice(None)) if i < 4 else (slice(None), place)
            copy = pltpu.make_async_copy(sources[i].at[at], held[i].at[at], sems.at[k, i % 4])
            copy.start()
            copies[k].append(copy)

    core, expert = info[2], info[5]
    rows = x[...].reshape(128, D)
    logits = lax.dot_general(
        rows, router[...], (((1,), (1,)), ((), ())), preferred_element_type=F32
    )
    r = lax.broadcasted_iota(jnp.int32, (128, SPAN), 0)
    u = lax.broadcasted_iota(jnp.int32, (128, SPAN), 1)
    token = (r % 16 // FINE * 2 + core) * BLOCK_TOKENS + r // 16 * FINE + r % FINE
    leading, trailing = ids[0:1, :], ids[1:2, :]
    chosen = (leading == expert) | (trailing == expert)
    other = jnp.where(leading == expert, trailing, leading)
    earlier = jnp.sum(jnp.where(chosen & (u < token), 1.0, 0.0), axis=1, keepdims=True)
    mine = jnp.sum(jnp.where(chosen & (u == token), 1.0, 0.0), axis=1, keepdims=True)
    other_id = jnp.sum(jnp.where(u == token, other.astype(F32), 0.0), axis=1, keepdims=True)
    lane = lax.broadcasted_iota(jnp.int32, logits.shape, 1)
    own_logit = jnp.sum(jnp.where(lane == expert, logits, 0.0), axis=1, keepdims=True)
    other_logit = jnp.sum(
        jnp.where(lane.astype(F32) == other_id, logits, 0.0), axis=1, keepdims=True
    )
    active = (mine > 0.5) & (earlier < CAP - 0.5)
    share = jnp.where(active, 1.0 / (1.0 + jnp.exp(other_logit - own_logit)), 0.0)

    sums = [jnp.zeros((128, units), F32)] * 4
    for k in range(MOE_PIECES):
        for copy in copies[k]:
            copy.wait()
        place = slice(k * MOE_TILE, (k + 1) * MOE_TILE)
        part = x[:, :, place].reshape(128, MOE_TILE)
        sums = [
            sums[i] + jnp.dot(part, held[i][place, :], preferred_element_type=F32) for i in range(4)
        ]
    hidden = [
        (sums[i] / (1.0 + jnp.exp(-sums[i])) * sums[i + 2]).astype(BF16) for i in range(2)
    ]
    for k in range(MOE_PIECES):
        for copy in copies[MOE_PIECES + k]:
            copy.wait()
        place = slice(k * MOE_TILE, (k + 1) * MOE_TILE)
        total = jnp.dot(hidden[0], held[4][:, place], preferred_element_type=F32)
        total = total + jnp.dot(hidden[1], held[5][:, place], preferred_element_type=F32)
        out[:, :, place] = (total * share).astype(BF16).reshape(NE, 16, MOE_TILE)


def experts(info, x, ids, router, *weights):
    units = weights[0].shape[1]
    return call(
        moe_kernel,
        (NE, 16, D),
        info,
        x,
        ids,
        router,
        *[in_hbm(w) for w in weights],
        specs=[SMEM] + [VMEM] * 3 + [ANY] * 6,
        limit=40,
        flops=6 * 128 * D * 512,
        scratch=[pltpu.VMEM((D, units), BF16)] * 4
        + [pltpu.VMEM((units, D), BF16)] * 2
        + [pltpu.SemaphoreType.DMA((2 * MOE_PIECES, 4))],
    )


def sum_kernel(parts, out):
    total = parts[0].astype(F32)
    for e in range(1, NE):
        total = total + parts[e].astype(F32)
    for z in range(NZ):
        out[z] = total[z * FINE : (z + 1) * FINE].astype(BF16)


def last_kernel(parts, own, out):
    total = own[:, :].astype(F32)[:FINE]
    for z in range(NZ):
        total = total + parts[z].astype(F32)
    out[...] = total.astype(BF16)


def shards(
    queries,
    span_keys,
    span_values,
    cache_keys,
    cache_values,
    span_start,
    residual,
    out_weight,
    norm_gain,
    router_weight,
    expert_ids,
    gate_weight,
    up_weight,
    down_weight,
):
    ctx_index = lax.axis_index("ctx")
    core = ctx_index % 2
    z_index = ctx_index // 2
    key_rows = cache_keys.shape[0]

    other_keys = sibling(cache_keys)
    other_values = sibling(cache_values)
    span_own = jnp.concatenate([span_keys, span_values], axis=1)
    other_span = sibling(span_own)
    message = call(
        first_message_kernel,
        (NZ, MESSAGE_ROWS, HEAD_DIM),
        in_hbm(queries),
        in_hbm(residual),
        space=pltpu.HBM,
    )
    first = exchange_z(message)
    other_out = sibling(out_weight)
    other_gate = sibling(gate_weight)
    other_up = sibling(up_weight)
    other_down = sibling(down_weight)

    def valid(index):
        return jnp.clip(span_start[0] - index * key_rows, 0, key_rows)

    own_first = core == 0
    span_both = jnp.concatenate(
        [jnp.where(own_first, span_own, other_span), jnp.where(own_first, other_span, span_own)], axis=0
    )
    info = jnp.stack(
        [
            valid(ctx_index),
            valid(ctx_index ^ 1),
            core,
            z_index * 2 * BLOCK_TOKENS,
            z_index,
            z_index // 2,
        ]
    ).astype(jnp.int32)
    prepared_values, prepared_keys = prepare(in_hbm(cache_values), other_values, other_keys)
    partial = call(
        attention_kernel,
        (NZ, MESSAGE_ROWS, HEAD_DIM),
        info,
        first,
        in_hbm(cache_keys),
        in_hbm(prepared_keys),
        in_hbm(prepared_values),
        span_both[:, :HEAD_DIM],
        span_both[:, HEAD_DIM:],
        specs=[SMEM, VMEM, ANY, ANY, ANY, VMEM, VMEM],
        space=pltpu.HBM,
        limit=48,
        flops=64 * ROWS * 2 * CHUNK * HEAD_DIM,
        scratch=[
            pltpu.VMEM((ROWS, HEAD_DIM), BF16),
            pltpu.VMEM((2, CHUNK, HEAD_DIM), BF16),
            pltpu.VMEM((2, HEAD_DIM + 16, CHUNK), BF16),
            pltpu.VMEM((8, ROWS), F32),
            pltpu.VMEM((HEAD_DIM + 16, ROWS), F32),
            pltpu.SemaphoreType.DMA((4,)),
            pltpu.SMEM((1,), jnp.int32),
        ],
    )
    second = exchange_z(partial)
    attended, other_out, gain = call_and_pass(
        combine_kernel,
        (NZ, BLOCK_TOKENS, COLS),
        (second,),
        (in_vmem(other_out), in_hbm(norm_gain.reshape(1, D))),
    )
    third = exchange_z(attended)
    fourth = exchange_exp(
        call(
            project_kernel,
            (NE, 16, COLS),
            info,
            third,
            out_weight,
            other_out,
            specs=[SMEM, VMEM, VMEM, VMEM],
        )
    )
    fifth = exchange_z(call(mid_kernel, (NZ, 16, COLS), fourth, first))
    passed = [in_hbm(w) for w in (other_gate, other_up, other_down)]
    normed, own_mid, other_gate, other_up, other_down = pl.pallas_call(
        norm_kernel,
        out_shape=[
            jax.ShapeDtypeStruct((NE, 16, D), BF16),
            jax.ShapeDtypeStruct((16, D), BF16),
        ]
        + [jax.ShapeDtypeStruct(w.shape, w.dtype) for w in passed],
        in_specs=[SMEM, VMEM, VMEM, ANY, ANY, ANY],
        out_specs=[VMEM, VMEM, ANY, ANY, ANY],
        input_output_aliases={3: 2, 4: 3, 5: 4},
        compiler_params=pltpu.CompilerParams(vmem_limit_bytes=16 << 20),
        cost_estimate=pl.CostEstimate(flops=1 << 20, bytes_accessed=2 << 20, transcendentals=0),
    )(info, fifth, gain, *passed)
    tokens = exchange_exp(normed)

    result = experts(
        info,
        tokens,
        expert_ids.T,
        router_weight.T,
        gate_weight,
        other_gate,
        up_weight,
        other_up,
        down_weight,
        other_down,
    )
    sixth = exchange_exp(result)
    seventh = exchange_z(call(sum_kernel, (NZ, FINE, D), sixth))
    return call(last_kernel, (FINE, D), seventh, own_mid)


def solution(mesh):
    placed = (
        P(("dp", "ctx"), "exp"),
        P(("dp", "ctx"), "exp"),
        P(("dp", "ctx"), "exp"),
        P(("dp", "ctx"), "exp"),
        P(("dp", "ctx"), "exp"),
        P("dp"),
        P(("dp", "ctx", "exp"), None),
        P("exp", "ctx"),
        P(),
        P(),
        P("dp", None),
        P(None, ("ctx", "exp")),
        P(None, ("ctx", "exp")),
        P(("ctx", "exp"), None),
    )
    return jax.shard_map(
        shards, mesh=mesh, in_specs=placed, out_specs=P(("dp", "ctx", "exp"), None), check_vma=False
    )
```

```python
import math

import jax
import jax.numpy as jnp
from jax import lax
from jax.experimental import pallas as pl
from jax.experimental.pallas import tpu as pltpu
from jax.sharding import PartitionSpec as P

D = 6144
HEAD_DIM = 128
EXPERTS = 4
FF = 8192
TOPK = 2
SPAN = 256
CAP = 160
NZ = 8
NE = 8
FINE = 2
HEADS_LOCAL = 6
BLOCK_TOKENS = 16
BLOCK_ROWS = BLOCK_TOKENS * HEADS_LOCAL
ROWS = NZ * BLOCK_ROWS
Q_BLOCK = 256
CHUNK = 4096
NEAR = 256
FAR = 2.0**64
MESSAGE_ROWS = BLOCK_ROWS + 16
COLS = 768
HALF = 384
EPSILON = 1e-05
MASKED = -1e30
EXP2_SCALE = HEAD_DIM**-0.5 * math.log2(math.e)
BF16 = jnp.bfloat16
F32 = jnp.float32

Z_GROUPS = [[2 * z + core for z in range(NZ)] for core in range(2)]
SIBLINGS = [(c, c ^ 1) for c in range(2 * NZ)]


def exchange_z(blocks):
    return lax.all_to_all(blocks, "ctx", 0, 0, axis_index_groups=Z_GROUPS, tiled=True)


def exchange_exp(blocks):
    return lax.all_to_all(blocks, "exp", 0, 0, tiled=True)


def sibling(x):
    return lax.ppermute(x, "ctx", SIBLINGS)


VMEM = pl.BlockSpec(memory_space=pltpu.VMEM)
SMEM = pl.BlockSpec(memory_space=pltpu.SMEM)
ANY = pl.BlockSpec(memory_space=pl.ANY)


def in_hbm(x):
    return pltpu.with_memory_space_constraint(x, pltpu.HBM)


def in_vmem(x):
    return pltpu.with_memory_space_constraint(x, pltpu.VMEM)


def call(
    kernel,
    shape,
    *args,
    specs=None,
    space=jax.ShapeDtypeStruct,
    limit=32,
    flops=1 << 20,
    scratch=(),
):
    return pl.pallas_call(
        kernel,
        out_shape=space(shape, BF16),
        in_specs=specs or [VMEM] * len(args),
        out_specs=VMEM,
        scratch_shapes=scratch,
        compiler_params=pltpu.CompilerParams(vmem_limit_bytes=limit << 20),
        cost_estimate=pl.CostEstimate(flops=flops, bytes_accessed=1 << 20, transcendentals=0),
    )(*args)


def first_message_kernel(q, residual, span_keys, span_values, out, span):
    span[:, :HEAD_DIM] = span_keys[...]
    span[:, HEAD_DIM:] = span_values[...]
    res = residual[...].astype(F32)
    row = lax.broadcasted_iota(jnp.int32, (16, HEAD_DIM), 0)
    for z in range(NZ):
        for h in range(HEADS_LOCAL):
            out[z, h * BLOCK_TOKENS : (h + 1) * BLOCK_TOKENS, :] = q[
                :, h * HEAD_DIM : (h + 1) * HEAD_DIM
            ]
        rows = jnp.zeros((16, HEAD_DIM), F32)
        for j in range(COLS // HEAD_DIM):
            start = z * COLS + j * HEAD_DIM
            piece = res[:, start : start + HEAD_DIM]
            for f in range(FINE):
                rows = jnp.where(row == j * FINE + f, piece[f : f + 1, :], rows)
        out[z, BLOCK_ROWS:, :] = rows.astype(BF16)


def split3(x):
    first = x.astype(BF16).astype(F32)
    rest = x - first
    second = rest.astype(BF16).astype(F32)
    return first, second, rest - second


def prepare_kernel(v0, v1, k1, values, keys, sem):
    copy = pltpu.make_async_copy(k1, keys, sem)
    copy.start()
    for part, rows in enumerate((v0, v1)):
        values[part, :HEAD_DIM, :] = rows[...].T
        values[part, HEAD_DIM:, :] = jnp.ones((16, CHUNK), BF16)
    copy.wait()


def prepare(v0, v1, k1):
    return pl.pallas_call(
        prepare_kernel,
        out_shape=(
            pltpu.HBM((2, HEAD_DIM + 16, CHUNK), BF16),
            pltpu.HBM((CHUNK, HEAD_DIM), BF16),
        ),
        in_specs=[VMEM, VMEM, ANY],
        out_specs=(VMEM, ANY),
        scratch_shapes=[pltpu.SemaphoreType.DMA],
        compiler_params=pltpu.CompilerParams(vmem_limit_bytes=16 << 20),
        cost_estimate=pl.CostEstimate(flops=0, bytes_accessed=6 << 20, transcendentals=0),
    )(v0, v1, k1)


def attention_kernel(
    info, first, k0, k1, turned, sk, sv, out, q, keys, values, peak, carried, sems, again
):
    copies = []
    for part, source in enumerate((k0, k1)):
        copies.append(pltpu.make_async_copy(source, keys.at[part], sems.at[2 * part]))
        copies.append(
            pltpu.make_async_copy(turned.at[part], values.at[part], sems.at[2 * part + 1])
        )
    for copy in copies:
        copy.start()
    q[...] = first[:, :BLOCK_ROWS, :].reshape(ROWS, HEAD_DIM)
    blocks = ROWS // Q_BLOCK

    def columns(b):
        return slice(b * Q_BLOCK, (b + 1) * Q_BLOCK)

    def scores_of(rows, b):
        return lax.dot_general(
            rows, q[columns(b), :], (((1,), (1,)), ((), ())), preferred_element_type=F32
        )

    core = info[2]
    span_rows = 2 * BLOCK_TOKENS
    mine, theirs = sk[...].astype(F32), sv[...].astype(F32)
    lead = (core == 0).astype(F32)
    pair = jnp.concatenate(
        [mine * lead + theirs * (1.0 - lead), theirs * lead + mine * (1.0 - lead)], axis=0
    ).astype(BF16)
    key_pair, value_pair = pair[:, :HEAD_DIM], pair[:, HEAD_DIM:]

    def begin():
        span_values = jnp.concatenate([value_pair.T, jnp.ones((16, span_rows), BF16)], axis=0)
        for b in range(blocks):
            row = lax.broadcasted_iota(jnp.int32, (span_rows, Q_BLOCK), 0)
            col = lax.broadcasted_iota(jnp.int32, (span_rows, Q_BLOCK), 1) + b * Q_BLOCK
            token = col // BLOCK_ROWS * span_rows + core * BLOCK_TOKENS + col % BLOCK_TOKENS
            allowed = info[3] + row <= token
            s = jnp.where(allowed, scores_of(key_pair, b), MASKED)
            top = jnp.max(s, axis=0, keepdims=True)
            w = jnp.where(allowed, jnp.exp2((s - top) * EXP2_SCALE), 0.0).astype(BF16)
            peak[:, columns(b)] = jnp.broadcast_to(top, (8, Q_BLOCK))
            carried[:, columns(b)] = jnp.dot(span_values, w, preferred_element_type=F32)

    def soften(s, b):
        before = peak[:1, columns(b)]
        top = jnp.maximum(before, jnp.max(s, axis=0, keepdims=True))
        peak[:, columns(b)] = jnp.broadcast_to(top, (8, Q_BLOCK))
        w = jnp.exp2((s - top) * EXP2_SCALE).astype(BF16)
        return w, jnp.exp2((before - top) * EXP2_SCALE)

    def soften_near(s, b, part):
        before = top = peak[:1, columns(b)]
        factor = None
        if part == 0:
            top = jnp.maximum(before, jnp.max(s[:NEAR], axis=0, keepdims=True))
            peak[:, columns(b)] = jnp.broadcast_to(top, (8, Q_BLOCK))
            factor = jnp.exp2((before - top) * EXP2_SCALE)
        return jnp.exp2((s - top) * EXP2_SCALE).astype(BF16), factor

    def run(parts, count, valid=None, near=False, wait=lambda i: None):
        items = [(part, b) for part in parts for b in range(blocks)]

        def scores(item):
            s = scores_of(keys[item[0], :count, :], item[1])
            if valid is not None:
                row = lax.broadcasted_iota(jnp.int32, (count, Q_BLOCK), 0)
                s = jnp.where(row < valid, s, MASKED)
            return s

        def gather(item, w, factor):
            part, b = item
            sums = jnp.dot(values[part, :, :count], w, preferred_element_type=F32)
            held = carried[:, columns(b)]
            carried[:, columns(b)] = (held if factor is None else held * factor) + sums

        wait(0)
        s, later = scores(items[0]), scores(items[1])
        wait(1)
        earlier = None
        for i, item in enumerate(items):
            if i > 0:
                later = scores(items[i + 1]) if i + 1 < len(items) else None
            current = soften_near(s, item[1], item[0]) if near else soften(s, item[1])
            if earlier is not None:
                gather(items[i - 1], *earlier)
            earlier, s = current, later
        gather(items[-1], *earlier)

    def wait_for(stage):
        for copy in copies[:1] if stage == 0 else copies[1:]:
            copy.wait()

    begin()
    everything = (info[0] == CHUNK) & (info[1] == CHUNK)
    again[0] = jnp.int32(1)

    @pl.when(everything)
    def _():
        run((0, 1), CHUNK, near=True, wait=wait_for)
        mass = carried[HEAD_DIM : HEAD_DIM + 1, :]
        far = jnp.max(jnp.where(mass < FAR, 0.0, 1.0))
        again[0] = (far > 0.5).astype(jnp.int32)

        @pl.when(again[0] == 1)
        def _():
            begin()

    @pl.when(jnp.logical_not(everything))
    def _():
        wait_for(0)
        wait_for(1)

    @pl.when(again[0] == 1)
    def _():
        @pl.loop(0, 2)
        def _(part):
            valid = info[part]

            @pl.when(valid == CHUNK)
            def _():
                run((part,), CHUNK)

            @pl.when((valid < CHUNK) & (valid > CHUNK // 2))
            def _():
                run((part,), CHUNK, valid)

            @pl.when((valid <= CHUNK // 2) & (valid > 0))
            def _():
                run((part,), CHUNK // 2, valid)

    rows = carried[:HEAD_DIM, :].T.astype(BF16)
    out[:, :BLOCK_ROWS, :] = rows.reshape(NZ, BLOCK_ROWS, HEAD_DIM)
    terms = split3(peak[:1, :]) + split3(carried[HEAD_DIM : HEAD_DIM + 1, :])
    row = lax.broadcasted_iota(jnp.int32, (16, ROWS), 0)
    stats = jnp.zeros((16, ROWS), F32)
    for i, term in enumerate(terms):
        stats = jnp.where(row == i, term, stats)
    for z in range(NZ):
        shifted = stats if z == 0 else pltpu.roll(stats, ROWS - z * BLOCK_ROWS, 1)
        out[z, BLOCK_ROWS:, :] = shifted[:, :HEAD_DIM].astype(BF16)


def combine_kernel(message, *refs):
    out = refs[len(refs) // 2]
    peaks, masses = [], []
    for z in range(NZ):
        r = message[z, BLOCK_ROWS:, :].astype(F32)
        peaks.append(r[0:1] + r[1:2] + r[2:3])
        masses.append(r[3:4] + r[4:5] + r[5:6])
    top = peaks[0]
    for z in range(1, NZ):
        top = jnp.maximum(top, peaks[z])
    factors = [jnp.exp2((p - top) * EXP2_SCALE) for p in peaks]
    total = factors[0] * masses[0]
    for z in range(1, NZ):
        total = total + factors[z] * masses[z]
    row = lax.broadcasted_iota(jnp.int32, (HEAD_DIM, HEAD_DIM), 0)
    shares = jnp.zeros((HEAD_DIM, HEAD_DIM), F32)
    for z in range(NZ):
        shares = jnp.where(row == z, factors[z] / total, shares)
    shares = shares.T
    rows = jnp.zeros((BLOCK_ROWS, HEAD_DIM), F32)
    for z in range(NZ):
        rows = rows + message[z, :BLOCK_ROWS, :].astype(F32) * shares[:BLOCK_ROWS, z : z + 1]
    rows = rows.astype(BF16)
    for h in range(HEADS_LOCAL):
        piece = rows[h * BLOCK_TOKENS : (h + 1) * BLOCK_TOKENS]
        for z in range(NZ):
            out[z, :, h * HEAD_DIM : (h + 1) * HEAD_DIM] = piece


def call_and_pass(kernel, shape, args, carried):
    count, first = len(carried), len(args)
    return pl.pallas_call(
        kernel,
        out_shape=[jax.ShapeDtypeStruct(shape, BF16)]
        + [jax.ShapeDtypeStruct(c.shape, c.dtype) for c in carried],
        in_specs=[VMEM] * first + [ANY] * count,
        out_specs=[VMEM] + [ANY] * count,
        input_output_aliases={first + i: 1 + i for i in range(count)},
        compiler_params=pltpu.CompilerParams(vmem_limit_bytes=16 << 20),
        cost_estimate=pl.CostEstimate(flops=1 << 20, bytes_accessed=1 << 20, transcendentals=0),
    )(*args, *carried)


def project_kernel(info, x, own, other, out):
    r = lax.broadcasted_iota(jnp.int32, (128, 128), 0)
    c = lax.broadcasted_iota(jnp.int32, (128, 128), 1)
    wanted = r % 16 // FINE * 16 + r // 16 * FINE + r % FINE
    turn = jnp.where(c == wanted, 1.0, 0.0).astype(BF16)
    rows = jnp.dot(turn, x[...].reshape(128, COLS), preferred_element_type=F32).astype(BF16)
    core = info[2]
    for weight, side in ((own, core), (other, 1 - core)):
        part = jnp.dot(rows, weight[...], preferred_element_type=F32).astype(BF16)
        out[:, :, pl.ds(pl.multiple_of(side * HALF, HALF), HALF)] = part.reshape(NE, 16, HALF)


def mid_kernel(parts, message, out):
    total = parts[0].astype(F32)
    for e in range(1, NE):
        total = total + parts[e].astype(F32)
    rows = message[:, BLOCK_ROWS:, :].reshape(128, HEAD_DIM)
    r = lax.broadcasted_iota(jnp.int32, (16, 128), 0)
    c = lax.broadcasted_iota(jnp.int32, (16, 128), 1)
    for j in range(COLS // HEAD_DIM):
        pick = jnp.where(c == r // FINE * 16 + j * FINE + r % FINE, 1.0, 0.0).astype(BF16)
        place = slice(j * HEAD_DIM, (j + 1) * HEAD_DIM)
        res = jnp.dot(pick, rows, preferred_element_type=F32)
        mid = (res + total[:, place]).astype(BF16)
        for z in range(NZ):
            out[z, :, place] = mid


def norm_kernel(info, parts, gain, *refs):
    out, own = refs[len(refs) // 2 - 1 : len(refs) // 2 + 1]
    squares = jnp.zeros((16, 1), F32)
    for z in range(NZ):
        wide = parts[z].astype(F32)
        squares = squares + jnp.sum(wide * wide, axis=1, keepdims=True)
    scale = lax.rsqrt(squares * (1.0 / D) + EPSILON)
    r = lax.broadcasted_iota(jnp.int32, (16, 16), 0)
    c = lax.broadcasted_iota(jnp.int32, (16, 16), 1)
    pick = jnp.where((c == info[4] * FINE + r) & (r < FINE), 1.0, 0.0).astype(BF16)
    for z in range(NZ):
        place = slice(z * COLS, (z + 1) * COLS)
        mid = parts[z]
        normed = (mid.astype(F32) * scale * gain[:, place].astype(F32)).astype(BF16)
        for e in range(NE):
            out[e, :, place] = normed
        own[:, place] = jnp.dot(pick, mid, preferred_element_type=F32).astype(BF16)


MOE_PIECES = 4
MOE_TILE = D // MOE_PIECES


def moe_kernel(info, x, ids, router, *refs):
    sources, out, held, sems = refs[:6], refs[6], refs[7:13], refs[13]
    units = sources[0].shape[1]
    copies = []
    for k in range(2 * MOE_PIECES):
        place = pl.ds(k % MOE_PIECES * MOE_TILE, MOE_TILE)
        group = range(4) if k < MOE_PIECES else range(4, 6)
        copies.append([])
        for i in group:
            at = (place, slice(None)) if i < 4 else (slice(None), place)
            copy = pltpu.make_async_copy(sources[i].at[at], held[i].at[at], sems.at[k, i % 4])
            copy.start()
            copies[k].append(copy)

    core, expert = info[2], info[5]
    rows = x[...].reshape(128, D)
    logits = lax.dot_general(
        rows, router[...], (((1,), (1,)), ((), ())), preferred_element_type=F32
    )
    r = lax.broadcasted_iota(jnp.int32, (128, SPAN), 0)
    u = lax.broadcasted_iota(jnp.int32, (128, SPAN), 1)
    token = (r % 16 // FINE * 2 + core) * BLOCK_TOKENS + r // 16 * FINE + r % FINE
    leading, trailing = ids[0:1, :], ids[1:2, :]
    chosen = (leading == expert) | (trailing == expert)
    other = jnp.where(leading == expert, trailing, leading)
    earlier = jnp.sum(jnp.where(chosen & (u < token), 1.0, 0.0), axis=1, keepdims=True)
    mine = jnp.sum(jnp.where(chosen & (u == token), 1.0, 0.0), axis=1, keepdims=True)
    other_id = jnp.sum(jnp.where(u == token, other.astype(F32), 0.0), axis=1, keepdims=True)
    lane = lax.broadcasted_iota(jnp.int32, logits.shape, 1)
    own_logit = jnp.sum(jnp.where(lane == expert, logits, 0.0), axis=1, keepdims=True)
    other_logit = jnp.sum(
        jnp.where(lane.astype(F32) == other_id, logits, 0.0), axis=1, keepdims=True
    )
    active = (mine > 0.5) & (earlier < CAP - 0.5)
    share = jnp.where(active, 1.0 / (1.0 + jnp.exp(other_logit - own_logit)), 0.0)

    sums = [jnp.zeros((128, units), F32)] * 4
    for k in range(MOE_PIECES):
        for copy in copies[k]:
            copy.wait()
        place = slice(k * MOE_TILE, (k + 1) * MOE_TILE)
        part = x[:, :, place].reshape(128, MOE_TILE)
        sums = [
            sums[i] + jnp.dot(part, held[i][place, :], preferred_element_type=F32) for i in range(4)
        ]
    hidden = [
        (sums[i] / (1.0 + jnp.exp(-sums[i])) * sums[i + 2]).astype(BF16) for i in range(2)
    ]
    for k in range(MOE_PIECES):
        for copy in copies[MOE_PIECES + k]:
            copy.wait()
        place = slice(k * MOE_TILE, (k + 1) * MOE_TILE)
        total = jnp.dot(hidden[0], held[4][:, place], preferred_element_type=F32)
        total = total + jnp.dot(hidden[1], held[5][:, place], preferred_element_type=F32)
        out[:, :, place] = (total * share).astype(BF16).reshape(NE, 16, MOE_TILE)


def experts(info, x, ids, router, *weights):
    units = weights[0].shape[1]
    return call(
        moe_kernel,
        (NE, 16, D),
        info,
        x,
        ids,
        router,
        *[in_hbm(w) for w in weights],
        specs=[SMEM] + [VMEM] * 3 + [ANY] * 6,
        limit=40,
        flops=6 * 128 * D * 512,
        scratch=[pltpu.VMEM((D, units), BF16)] * 4
        + [pltpu.VMEM((units, D), BF16)] * 2
        + [pltpu.SemaphoreType.DMA((2 * MOE_PIECES, 4))],
    )


def sum_kernel(parts, out):
    total = parts[0].astype(F32)
    for e in range(1, NE):
        total = total + parts[e].astype(F32)
    for z in range(NZ):
        out[z] = total[z * FINE : (z + 1) * FINE].astype(BF16)


def last_kernel(parts, own, out):
    total = own[:, :].astype(F32)[:FINE]
    for z in range(NZ):
        total = total + parts[z].astype(F32)
    out[...] = total.astype(BF16)


def shards(
    queries,
    span_keys,
    span_values,
    cache_keys,
    cache_values,
    span_start,
    residual,
    out_weight,
    norm_gain,
    router_weight,
    expert_ids,
    gate_weight,
    up_weight,
    down_weight,
):
    ctx_index = lax.axis_index("ctx")
    core = ctx_index % 2
    z_index = ctx_index // 2
    key_rows = cache_keys.shape[0]

    other_keys = sibling(cache_keys)
    other_values = sibling(cache_values)
    message, span_own = pl.pallas_call(
        first_message_kernel,
        out_shape=(
            pltpu.HBM((NZ, MESSAGE_ROWS, HEAD_DIM), BF16),
            jax.ShapeDtypeStruct((BLOCK_TOKENS, 2 * HEAD_DIM), BF16),
        ),
        in_specs=[VMEM] * 4,
        out_specs=(VMEM, VMEM),
        compiler_params=pltpu.CompilerParams(vmem_limit_bytes=32 << 20),
        cost_estimate=pl.CostEstimate(flops=1 << 20, bytes_accessed=1 << 20, transcendentals=0),
    )(in_hbm(queries), in_hbm(residual), in_hbm(span_keys), in_hbm(span_values))
    other_span = sibling(span_own)
    first = exchange_z(message)
    other_out = sibling(out_weight)
    other_gate = sibling(gate_weight)
    other_up = sibling(up_weight)
    other_down = sibling(down_weight)

    def valid(index):
        return jnp.clip(span_start[0] - index * key_rows, 0, key_rows)

    info = jnp.stack(
        [
            valid(ctx_index),
            valid(ctx_index ^ 1),
            core,
            z_index * 2 * BLOCK_TOKENS,
            z_index,
            z_index // 2,
        ]
    ).astype(jnp.int32)
    prepared_values, prepared_keys = prepare(in_hbm(cache_values), other_values, other_keys)
    partial = call(
        attention_kernel,
        (NZ, MESSAGE_ROWS, HEAD_DIM),
        info,
        first,
        in_hbm(cache_keys),
        in_hbm(prepared_keys),
        in_hbm(prepared_values),
        span_own,
        other_span,
        specs=[SMEM, VMEM, ANY, ANY, ANY, VMEM, VMEM],
        space=pltpu.HBM,
        limit=48,
        flops=64 * ROWS * 2 * CHUNK * HEAD_DIM,
        scratch=[
            pltpu.VMEM((ROWS, HEAD_DIM), BF16),
            pltpu.VMEM((2, CHUNK, HEAD_DIM), BF16),
            pltpu.VMEM((2, HEAD_DIM + 16, CHUNK), BF16),
            pltpu.VMEM((8, ROWS), F32),
            pltpu.VMEM((HEAD_DIM + 16, ROWS), F32),
            pltpu.SemaphoreType.DMA((4,)),
            pltpu.SMEM((1,), jnp.int32),
        ],
    )
    second = exchange_z(partial)
    attended, other_out, gain = call_and_pass(
        combine_kernel,
        (NZ, BLOCK_TOKENS, COLS),
        (second,),
        (in_vmem(other_out), in_hbm(norm_gain.reshape(1, D))),
    )
    third = exchange_z(attended)
    fourth = exchange_exp(
        call(
            project_kernel,
            (NE, 16, COLS),
            info,
            third,
            out_weight,
            other_out,
            specs=[SMEM, VMEM, VMEM, VMEM],
        )
    )
    fifth = exchange_z(call(mid_kernel, (NZ, 16, COLS), fourth, first))
    passed = [in_hbm(w) for w in (other_gate, other_up, other_down)]
    normed, own_mid, other_gate, other_up, other_down = pl.pallas_call(
        norm_kernel,
        out_shape=[
            jax.ShapeDtypeStruct((NE, 16, D), BF16),
            jax.ShapeDtypeStruct((16, D), BF16),
        ]
        + [jax.ShapeDtypeStruct(w.shape, w.dtype) for w in passed],
        in_specs=[SMEM, VMEM, VMEM, ANY, ANY, ANY],
        out_specs=[VMEM, VMEM, ANY, ANY, ANY],
        input_output_aliases={3: 2, 4: 3, 5: 4},
        compiler_params=pltpu.CompilerParams(vmem_limit_bytes=16 << 20),
        cost_estimate=pl.CostEstimate(flops=1 << 20, bytes_accessed=2 << 20, transcendentals=0),
    )(info, fifth, gain, *passed)
    tokens = exchange_exp(normed)

    result = experts(
        info,
        tokens,
        expert_ids.T,
        router_weight.T,
        gate_weight,
        other_gate,
        up_weight,
        other_up,
        down_weight,
        other_down,
    )
    sixth = exchange_exp(result)
    seventh = exchange_z(call(sum_kernel, (NZ, FINE, D), sixth))
    return call(last_kernel, (FINE, D), seventh, own_mid)


def solution(mesh):
    placed = (
        P(("dp", "ctx"), "exp"),
        P(("dp", "ctx"), "exp"),
        P(("dp", "ctx"), "exp"),
        P(("dp", "ctx"), "exp"),
        P(("dp", "ctx"), "exp"),
        P("dp"),
        P(("dp", "ctx", "exp"), None),
        P("exp", "ctx"),
        P(),
        P(),
        P("dp", None),
        P(None, ("ctx", "exp")),
        P(None, ("ctx", "exp")),
        P(("ctx", "exp"), None),
    )
    return jax.shard_map(
        shards, mesh=mesh, in_specs=placed, out_specs=P(("dp", "ctx", "exp"), None), check_vma=False
    )
```
